32 devices in a mesh: shot: 4 (over z), gx: 4 (over y, x), gy: 2 (over core).
Axes of the slice: x: 2, y: 2, z: 4, core: 2. Of those that a mesh axis runs over, the one named last changes fastest.
Arguments:
- wave_now: float32 [4, 4, 128, 64, 128], P('shot', None, 'gx', 'gy'), may hold values from -6 to 6
- wave_prev: float32 [4, 4, 128, 64, 128], P('shot', None, 'gx', 'gy'), may hold values from -6 to 6
- vel_coef: float32 [128, 64, 128], P('gx', 'gy'), may hold values from 0.08 to 0.18
- epsilon: float32 [128, 64, 128], P('gx', 'gy'), may hold values from 0.15 to 0.35
- delta: float32 [128, 64, 128], P('gx', 'gy'), may hold values from 0 to 0.15
- tilt: int32 [128, 64, 128], P('gx', 'gy'), may hold values from 0 to 60
- azimuth: int32 [128, 64, 128], P('gx', 'gy'), may hold values from 0 to 359
- aperture: int32 [4, 4, 2], P('shot', 'gx', 'gy'), may hold values 0 or 1
Outputs:
- wave_final: float32 [4, 4, 128, 64, 128], P('shot', None, 'gx', 'gy')
- image: float32 [128, 64, 128], P('gx', 'gy')
The draws below stay inside these ranges and needn't reach their ends.
All inputs are finite; a program needn't handle non-finite values. No bound on the sum of `aperture` on one device may be relied on, other than what follows from the above.
Results may differ from the reference program's by a relative error of at most 0.00002.
Values sent between devices are 32-bit elements; how exact they have to be, the bound alone decides.
No kernel may reach another device: no remote copies, remote signals or barrier semaphores. Data moves between devices by JAX's collectives and lax.ppermute only.
A program may use at most 128 MiB of HBM per device.

```python
import math
import jax
import jax.numpy as jnp

CX = 32
CY = 32
ITERS = 4
FIELDS = 4
SHOTS = 4
NX = 128
NY = 64
NZ = 128
TILES_X = 4
TILES_Y = 2


def place_ends(entries, rng, least, top_value):
    longest = entries.shape.index(max(entries.shape))
    spots = []
    for shift in (0, 1):
        where = [jax.random.randint(jax.random.fold_in(rng, axis), (), 0, length) for axis, length in enumerate(entries.shape)]
        where[longest] = (where[longest] + shift) % entries.shape[longest]
        spots.append(tuple(where))
    return entries.at[spots[0]].set(least).at[spots[1]].set(top_value)


def shard_levels(stream_key, shape, cuts, low, top_value):
    factor_of = 1.0
    for dim, blocks in cuts:
        draws = jax.random.uniform(jax.random.fold_in(jax.random.fold_in(stream_key, 6), dim), (blocks,), jnp.float32, low / len(cuts), top_value / len(cuts))
        factor_of = factor_of * jnp.repeat(jnp.exp(draws), shape[dim] // blocks).reshape((-1,) + (1,) * (len(shape) - 1 - dim))
    return factor_of


def centred(rng, shape, width, limit, split=(), kind=jnp.bfloat16):
    result = width * jax.random.normal(rng, shape, jnp.float32)
    if split:
        result = result * shard_levels(rng, shape, split, -0.22, 0.18)
    return jnp.clip(result, -limit, limit).astype(kind)


def setup_inputs(seed: int = 0) -> dict:
    streams_of = jax.random.split(jax.random.key(seed), 9)
    return {
        "wave_now": centred(streams_of[0], (SHOTS, FIELDS, NX, NY, NZ), 1.0, 6.0, ((0, 4), (2, 4), (3, 2)), jnp.float32),
        "wave_prev": centred(streams_of[1], (SHOTS, FIELDS, NX, NY, NZ), 1.0, 6.0, ((0, 4), (2, 4), (3, 2)), jnp.float32),
        "vel_coef": jnp.clip(jnp.exp(math.log(0.18) - 0.81093028 * jax.random.uniform(streams_of[2], (NX, NY, NZ), jnp.float32) ** shard_levels(streams_of[2], (NX, NY, NZ), ((0, 4), (1, 2)), -0.2, 0.2)), 0.08, 0.18),
        "epsilon": jnp.clip(0.15 + 0.19999999 * jax.random.uniform(streams_of[3], (NX, NY, NZ), jnp.float32) ** shard_levels(streams_of[3], (NX, NY, NZ), ((0, 4), (1, 2)), -0.2, 0.2), 0.15, 0.35),
        "delta": jnp.clip(0.15 * jax.random.uniform(streams_of[4], (NX, NY, NZ), jnp.float32) ** shard_levels(streams_of[4], (NX, NY, NZ), ((0, 4), (1, 2)), -0.2, 0.2), 0.0, 0.15),
        "tilt": place_ends(jax.random.randint(streams_of[5], (NX, NY, NZ), 0, 61), jax.random.fold_in(streams_of[5], 1), 0, 60).astype(jnp.int32),
        "azimuth": place_ends(jax.random.randint(streams_of[6], (NX, NY, NZ), 0, 360), jax.random.fold_in(streams_of[6], 1), 0, 359).astype(jnp.int32),
        "aperture": place_ends((jax.random.randint(streams_of[7], (SHOTS, TILES_X, TILES_Y), 0, 4) < 3).astype(jnp.int32), jax.random.fold_in(streams_of[7], 1), 0, 1),
    }


def model_terms(vel_coef, epsilon, delta, tilt, azimuth):
    theta = tilt.astype(jnp.float32) * (math.pi / 180.0)
    phi = azimuth.astype(jnp.float32) * (math.pi / 180.0)
    normal_x = jnp.sin(theta) * jnp.cos(phi)
    normal_y = jnp.sin(theta) * jnp.sin(phi)
    normal_z = jnp.cos(theta)
    gain = 1.0 + 2.0 * epsilon
    root = jnp.sqrt(1.0 + 2.0 * delta)
    return jnp.stack([normal_x, normal_y, normal_z, vel_coef, gain, root], axis=0)

def advance(padded, previous, coef):
    width_x = padded.shape[-3] - 2
    width_y = padded.shape[-2] - 2
    width_z = padded.shape[-1] - 2

    def shifted(off_x, off_y, off_z):
        return padded[..., 1 + off_x:1 + off_x + width_x, 1 + off_y:1 + off_y + width_y, 1 + off_z:1 + off_z + width_z]
    centre = shifted(0, 0, 0)
    second_x = shifted(1, 0, 0) + shifted(-1, 0, 0) - 2.0 * centre
    second_y = shifted(0, 1, 0) + shifted(0, -1, 0) - 2.0 * centre
    second_z = shifted(0, 0, 1) + shifted(0, 0, -1) - 2.0 * centre
    mixed_xy = 0.25 * (shifted(1, 1, 0) - shifted(1, -1, 0) - shifted(-1, 1, 0) + shifted(-1, -1, 0))
    mixed_xz = 0.25 * (shifted(1, 0, 1) - shifted(1, 0, -1) - shifted(-1, 0, 1) + shifted(-1, 0, -1))
    mixed_yz = 0.25 * (shifted(0, 1, 1) - shifted(0, 1, -1) - shifted(0, -1, 1) + shifted(0, -1, -1))
    normal_x, normal_y, normal_z = (coef[0], coef[1], coef[2])
    speed, gain, root = (coef[3], coef[4], coef[5])
    along = normal_x * normal_x * second_x + normal_y * normal_y * second_y + normal_z * normal_z * second_z + 2.0 * (normal_x * normal_y * mixed_xy + normal_x * normal_z * mixed_xz + normal_y * normal_z * mixed_yz)
    across = second_x + second_y + second_z - along
    pressure = centre[:, 0::2]
    auxiliary = centre[:, 1::2]
    rhs_p = gain * across[:, 0::2] + root * along[:, 1::2]
    rhs_q = root * across[:, 0::2] + along[:, 1::2]
    next_p = 2.0 * pressure - previous[:, 0::2] + speed * rhs_p
    next_q = 2.0 * auxiliary - previous[:, 1::2] + speed * rhs_q
    return jnp.stack([next_p, next_q], axis=2).reshape(centre.shape)

def reference(wave_now, wave_prev, vel_coef, epsilon, delta, tilt, azimuth, aperture):
    coef = model_terms(vel_coef, epsilon, delta, tilt, azimuth)
    finals = []
    image = jnp.zeros(vel_coef.shape, jnp.float32)
    for shot_index in range(SHOTS):
        current = wave_now[shot_index:shot_index + 1]
        previous = wave_prev[shot_index:shot_index + 1]
        correlation = jnp.zeros(vel_coef.shape, jnp.float32)
        for step in range(ITERS):
            padded = jnp.pad(current, ((0, 0), (0, 0), (1, 1), (1, 1), (1, 1)))
            fresh = advance(padded, previous, coef)
            correlation = correlation + fresh[0, 0] * fresh[0, 2]
            previous, current = (current, fresh)
        finals.append(current)
        covered = jnp.repeat(jnp.repeat(aperture[shot_index].astype(jnp.float32), CX, axis=0), CY, axis=1)
        image = image + covered[:, :, None] * correlation
    return (jnp.concatenate(finals, axis=0), image / ITERS)
```

```python
import functools
import math

import jax
import jax.numpy as jnp
from jax import lax
from jax.experimental import pallas as pl
from jax.experimental.pallas import tpu as pltpu
from jax.sharding import PartitionSpec as P

ITERS = 4
LANES = 128
TILE = 8
F32 = jnp.float32


def sin_cos(degrees):
    quadrant = jnp.floor(degrees * (1.0 / 90.0) + 0.5)
    angle = (degrees - 90.0 * quadrant) * (math.pi / 180.0)
    square = angle * angle
    sine = angle * (1.0 + square * (-1.0 / 6 + square * (1.0 / 120 + square * (-1.0 / 5040 + square * (1.0 / 362880)))))
    cosine = 1.0 + square * (
        -0.5 + square * (1.0 / 24 + square * (-1.0 / 720 + square * (1.0 / 40320 + square * (-1.0 / 3628800))))
    )
    turn = quadrant - 4.0 * jnp.floor(quadrant * 0.25)
    odd = (turn == 1.0) | (turn == 3.0)
    first = jnp.where(odd, cosine, sine)
    second = jnp.where(odd, sine, cosine)
    return (
        jnp.where(turn >= 2.0, -first, first),
        jnp.where((turn == 1.0) | (turn == 2.0), -second, second),
    )


def model_rows(vel, eps, delta, tilt, azimuth):
    sin_t, cos_t = sin_cos(tilt)
    sin_a, cos_a = sin_cos(azimuth)
    nx, ny, nz = sin_t * cos_a, sin_t * sin_a, cos_t
    gain = 1.0 + 2.0 * eps
    root = jnp.sqrt(1.0 + 2.0 * delta)
    return (
        nx * nx,
        ny * ny,
        nz * nz,
        0.5 * nx * ny,
        0.5 * nx * nz,
        0.5 * ny * nz,
        vel * gain,
        vel * root,
        vel,
    )


def sweep(src, dst, coef, corr, start, count, group, corr_scale=None):
    rows = coef.shape[2]
    lane = lax.broadcasted_iota(jnp.int32, (TILE, LANES), 1)
    first_lane, last_lane = lane == 0, lane == LANES - 1

    def neighbours(value):
        after = jnp.where(last_lane, 0.0, pltpu.roll(value, LANES - 1, 1))
        before = jnp.where(first_lane, 0.0, pltpu.roll(value, 1, 1))
        return after, before

    for pair in range(2):
        for tile in range(rows // TILE):
            row = TILE + tile * TILE

            def plane(field, x):
                centre = src[field, x, row : row + TILE, :]
                above = src[field, x, row + 1 : row + 1 + TILE, :]
                below = src[field, x, row - 1 : row - 1 + TILE, :]
                after, before = neighbours(centre)
                return centre, above - below, after - before, above + below, after + before

            def one(x, carry):
                terms = []
                following = []
                for index in range(2):
                    old, now = carry[index]
                    new = plane(2 * pair + index, x + 1)
                    a, b, c, d, e, g = [coef[i, x, row - TILE : row, :] for i in range(6)]
                    centre, slope_y, _, sum_y, sum_z = now
                    after, before = neighbours(slope_y)
                    twice = centre + centre
                    sum_x = new[0] + old[0]
                    along = (
                        (a * sum_x + b * sum_y)
                        + (c * sum_z - twice)
                        + (d * (new[1] - old[1]) + e * (new[2] - old[2]))
                        + g * (after - before)
                    )
                    laplace = (sum_x + sum_y) + (sum_z - 3.0 * twice) if index == 0 else None
                    terms.append((along, laplace, twice))
                    following.append((now[:3], new))
                (along_p, laplace, twice_p), (along_q, _, twice_q) = terms
                across = laplace - along_p
                vg, vr, v = [coef[i, x, row - TILE : row, :] for i in range(6, 9)]
                p, q = 2 * pair, 2 * pair + 1
                here = (x, slice(row, row + TILE), slice(None))
                new_p = (twice_p - dst[(p,) + here]) + (vg * across + vr * along_q)
                new_q = (twice_q - dst[(q,) + here]) + (vr * across + v * along_q)
                dst[(p,) + here] = new_p
                dst[(q,) + here] = new_q
                if pair == 1:
                    spot = (x, slice(row - TILE, row), slice(None))
                    total = corr[spot] + dst[(0,) + here] * new_p
                    corr[spot] = total
                return tuple(following)

            carry = tuple(
                (plane(2 * pair + index, start - 1)[:3], plane(2 * pair + index, start)) for index in range(2)
            )
            loops = count // group if count > group else 0
            if loops:

                def body(i, carry):
                    for j in range(group):
                        carry = one(start + i * group + j, carry)
                    return carry

                carry = lax.fori_loop(0, loops, body, carry)
            for j in range(loops * group, count):
                carry = one(start + j, carry)


def own_row(second):
    return pl.multiple_of(TILE + TILE * second, TILE)


def copies(pairs, sems):
    out = []
    for i, (source, target) in enumerate(pairs):
        out.append(pltpu.make_async_copy(source, target, sems.at[i]))
        out[-1].start()
    return out


def inner_kernel(
    flags, now, prev, vel, eps, delta, tilt, azimuth, border,
    wave, edge_a, edge_b, edge_c, edge_corr, image,
    buf_a, buf_b, coef, corr, raw, raw_int, raw_border, picture, sems,
):
    second, cover = flags[0], flags[1]
    width_x, width_y = vel.shape[0], vel.shape[1]
    oy = own_row(second)
    hy = pl.multiple_of(TILE + width_y * (1 - second), TILE)
    own = pl.ds(oy, width_y)
    hal = pl.ds(hy, TILE)
    model = copies(
        [
            (vel, raw.at[0]),
            (eps, raw.at[1]),
            (delta, raw.at[2]),
            (tilt, raw_int.at[0]),
            (azimuth, raw_int.at[1]),
            (border.at[pl.ds(8, 5)], raw_border),
        ],
        sems,
    )
    waves = copies(
        [
            (now.at[0], buf_a.at[:, :, own]),
            (prev.at[0], buf_b.at[:, :, own]),
            (border.at[pl.ds(0, 4)], buf_a.at[:, :, hal]),
            (border.at[pl.ds(4, 4)], buf_b.at[:, :, hal]),
        ],
        sems.at[pl.ds(6, 4)],
    )
    pad = jnp.zeros((4, width_x, TILE, LANES), F32)
    for buf in (buf_a, buf_b):
        buf[:, :, 0:TILE, :] = pad
        buf[:, :, TILE + coef.shape[2] :, :] = pad
    corr[...] = jnp.zeros_like(corr)
    for copy in model:
        copy.wait()

    def fill(x, _):
        for tile in range(width_y // TILE):
            rows = slice(tile * TILE, (tile + 1) * TILE)
            parts = model_rows(
                raw[0, x, rows, :],
                raw[1, x, rows, :],
                raw[2, x, rows, :],
                raw_int[0, x, rows, :].astype(F32),
                raw_int[1, x, rows, :].astype(F32),
            )
            for i, part in enumerate(parts):
                coef[i, x, pl.ds(oy - TILE + tile * TILE, TILE), :] = part
        parts = model_rows(*[raw_border[i, x] for i in range(5)])
        for i, part in enumerate(parts):
            coef[i, x, pl.ds(hy - TILE, TILE), :] = part
        return 0

    lax.fori_loop(0, width_x, fill, 0)
    for copy in waves:
        copy.wait()
    bufs = (buf_a, buf_b)
    for step in range(ITERS):
        sweep(bufs[step % 2], bufs[1 - step % 2], coef, corr, 1 + step, width_x - 2 - 2 * step, 3)
    last = bufs[ITERS % 2]
    inside = pl.ds(ITERS, width_x - 2 * ITERS)
    ends = (0, width_x - ITERS)
    pairs = [(last.at[:, inside, own], wave.at[0, :, inside])]
    middle = pl.ds(TILE, coef.shape[2])
    for side in range(2):
        at = pl.ds(ends[side], ITERS)
        wider = pl.ds(ends[side] - side, ITERS + 1)
        pairs += [
            (buf_a.at[:, at, middle], edge_a.at[side]),
            (buf_b.at[:, wider, middle], edge_b.at[side]),
            (coef.at[:, at], edge_c.at[side]),
            (corr.at[at], edge_corr.at[side]),
        ]
    out = copies(pairs, sems)
    scale = cover.astype(F32) / ITERS
    for tile in range(width_y // TILE):
        rows = pl.ds(oy - TILE + tile * TILE, TILE)
        picture[:, tile * TILE : (tile + 1) * TILE, :] = scale * corr[ITERS : width_x - ITERS, rows, :]
    final = pltpu.make_async_copy(picture, image, sems.at[len(pairs)])
    final.start()
    for copy in out:
        copy.wait()
    final.wait()


def border_kernel(
    flags, edge_a, edge_b, edge_c, edge_corr, halo, corner, wave_in,
    wave, image,
    buf_a, buf_b, coef, corr, raw, raw_corner, picture, sems,
):
    second, cover = flags[0], flags[1]
    width_x, width_y = wave.shape[2], wave.shape[3]
    oy = own_row(second)
    hy = pl.multiple_of(TILE + width_y * (1 - second), TILE)
    own = pl.ds(oy, width_y)
    hal = pl.ds(hy, TILE)
    middle = pl.ds(TILE, coef.shape[2])
    fields = 4
    n_now, n_prev = fields * ITERS, fields * (ITERS - 1)
    scale = cover.astype(F32) / ITERS
    pad = jnp.zeros((4, buf_a.shape[1], TILE, LANES), F32)
    for buf in (buf_a, buf_b):
        buf[:, :, 0:TILE, :] = pad
        buf[:, :, TILE + coef.shape[2] :, :] = pad
    for side in range(2):
        own_a, own_b = (ITERS, ITERS) if side == 0 else (1, 0)
        halo_a, halo_b = (0, 1) if side == 0 else (ITERS + 1, ITERS + 1)
        pairs = [
            (edge_a.at[side], buf_a.at[:, pl.ds(own_a, ITERS), middle]),
            (edge_b.at[side], buf_b.at[:, pl.ds(own_b, ITERS + 1), middle]),
            (edge_c.at[side], coef.at[:, pl.ds(own_a, ITERS)]),
            (edge_corr.at[side], corr.at[pl.ds(own_a, ITERS)]),
            (halo.at[side, pl.ds(n_now + n_prev, 5 * (ITERS - 1))], raw),
            (corner.at[side, pl.ds(n_now + n_prev, 5 * (ITERS - 1))], raw_corner),
        ]
        for f in range(fields):
            pairs += [
                (halo.at[side, pl.ds(f * ITERS, ITERS)], buf_a.at[f, pl.ds(halo_a, ITERS), own]),
                (corner.at[side, pl.ds(f * ITERS, ITERS)], buf_a.at[f, pl.ds(halo_a, ITERS), hal]),
                (
                    halo.at[side, pl.ds(n_now + f * (ITERS - 1), ITERS - 1)],
                    buf_b.at[f, pl.ds(halo_b, ITERS - 1), own],
                ),
                (
                    corner.at[side, pl.ds(n_now + f * (ITERS - 1), ITERS - 1)],
                    buf_b.at[f, pl.ds(halo_b, ITERS - 1), hal],
                ),
            ]
        for copy in copies(pairs, sems):
            copy.wait()
        for j in range(ITERS - 1):
            for tile in range(width_y // TILE):
                rows = slice(tile * TILE, (tile + 1) * TILE)
                parts = model_rows(*[raw[i * (ITERS - 1) + j, rows, :] for i in range(5)])
                for i, part in enumerate(parts):
                    coef[i, halo_b + j, pl.ds(oy - TILE + tile * TILE, TILE), :] = part
            parts = model_rows(*[raw_corner[i * (ITERS - 1) + j] for i in range(5)])
            for i, part in enumerate(parts):
                coef[i, halo_b + j, pl.ds(hy - TILE, TILE), :] = part
        bufs = (buf_a, buf_b)
        for step in range(ITERS):
            start = step + 1 if side == 0 else ITERS - step
            sweep(bufs[step % 2], bufs[1 - step % 2], coef, corr, start, ITERS, ITERS)
        last = bufs[ITERS % 2]
        for tile in range(width_y // TILE):
            rows = pl.ds(oy - TILE + tile * TILE, TILE)
            picture[side, :, tile * TILE : (tile + 1) * TILE, :] = scale * corr[own_a : own_a + ITERS, rows, :]
        target = pl.ds(0 if side == 0 else width_x - ITERS, ITERS)
        for copy in copies(
            [
                (last.at[:, pl.ds(own_a, ITERS), own], wave.at[0, :, target]),
                (picture.at[side], image.at[side]),
            ],
            sems,
        ):
            copy.wait()


def any_specs(count):
    return [pl.BlockSpec(memory_space=pl.ANY)] * count


def advance_inner(flags, now, prev, vel, eps, delta, tilt, azimuth, border):
    width_x, width_y = vel.shape[0], vel.shape[1]
    rows = width_y + TILE
    tall = rows + 2 * TILE
    shape = functools.partial(jax.ShapeDtypeStruct, dtype=F32)
    return pl.pallas_call(
        inner_kernel,
        in_specs=[pl.BlockSpec(memory_space=pltpu.SMEM)] + any_specs(8),
        out_specs=any_specs(6),
        out_shape=(
            shape(now.shape),
            shape((2, 4, ITERS, rows, LANES)),
            shape((2, 4, ITERS + 1, rows, LANES)),
            shape((2, 9, ITERS, rows, LANES)),
            shape((2, ITERS, rows, LANES)),
            shape((width_x - 2 * ITERS, width_y, LANES)),
        ),
        scratch_shapes=[
            pltpu.VMEM((4, width_x, tall, LANES), F32),
            pltpu.VMEM((4, width_x, tall, LANES), F32),
            pltpu.VMEM((9, width_x, rows, LANES), F32),
            pltpu.VMEM((width_x, rows, LANES), F32),
            pltpu.VMEM((3, width_x, width_y, LANES), F32),
            pltpu.VMEM((2, width_x, width_y, LANES), jnp.int32),
            pltpu.VMEM((5, width_x, TILE, LANES), F32),
            pltpu.VMEM((width_x - 2 * ITERS, width_y, LANES), F32),
            pltpu.SemaphoreType.DMA((10,)),
        ],
        compiler_params=pltpu.CompilerParams(vmem_limit_bytes=40 * 1024 * 1024),
        cost_estimate=pl.CostEstimate(flops=80_000_000, bytes_accessed=16_000_000, transcendentals=0),
        name="inner_steps",
    )(flags, now, prev, vel, eps, delta, tilt, azimuth, border)


def advance_border(flags, edge_a, edge_b, edge_c, edge_corr, halo, corner, wave):
    width_y = wave.shape[3]
    rows = width_y + TILE
    tall = rows + 2 * TILE
    deep = 2 * ITERS + 1
    shape = functools.partial(jax.ShapeDtypeStruct, dtype=F32)
    return pl.pallas_call(
        border_kernel,
        in_specs=[pl.BlockSpec(memory_space=pltpu.SMEM)] + any_specs(7),
        out_specs=any_specs(2),
        out_shape=(shape(wave.shape), shape((2, ITERS, width_y, LANES))),
        scratch_shapes=[
            pltpu.VMEM((4, deep, tall, LANES), F32),
            pltpu.VMEM((4, deep, tall, LANES), F32),
            pltpu.VMEM((9, deep, rows, LANES), F32),
            pltpu.VMEM((deep, rows, LANES), F32),
            pltpu.VMEM((5 * (ITERS - 1), width_y, LANES), F32),
            pltpu.VMEM((5 * (ITERS - 1), TILE, LANES), F32),
            pltpu.VMEM((2, ITERS, width_y, LANES), F32),
            pltpu.SemaphoreType.DMA((22,)),
        ],
        input_output_aliases={7: 0},
        compiler_params=pltpu.CompilerParams(vmem_limit_bytes=40 * 1024 * 1024),
        cost_estimate=pl.CostEstimate(flops=20_000_000, bytes_accessed=4_000_000, transcendentals=0),
        name="border_steps",
    )(flags, edge_a, edge_b, edge_c, edge_corr, halo, corner, wave)


def cut(array, start, size, axis):
    return lax.dynamic_slice_in_dim(array, start, size, axis=axis)


def swap_y(block, axis, second):
    start = (1 - second) * (block.shape[axis] - TILE)
    return lax.ppermute(cut(block, start, TILE, axis), "gy", [(0, 1), (1, 0)])


def face(now, prev, model, low):
    width_x = now.shape[1]
    parts = []
    for group, size in ((now, ITERS), (prev, ITERS - 1), (model, ITERS - 1)):
        at = 0 if low else width_x - size
        part = lax.slice_in_dim(group, at, at + size, axis=1)
        parts.append(part.reshape((-1,) + part.shape[2:]))
    return jnp.concatenate(parts, axis=0)


def sum_shots(block):
    count = lax.axis_size("shot")
    distance = 1
    while distance < count:
        block = block + lax.ppermute(block, "shot", [(i, i ^ distance) for i in range(count)])
        distance *= 2
    return block


def sum_shots_halves(block):
    count = lax.axis_size("shot")
    part = block.shape[0] // 2
    odd = lax.axis_index("shot") % 2
    near = [(i, i ^ 1) for i in range(count)]
    held = cut(block, odd * part, part, 0) + lax.ppermute(cut(block, (1 - odd) * part, part, 0), "shot", near)
    distance = 2
    while distance < count:
        held = held + lax.ppermute(held, "shot", [(i, i ^ distance) for i in range(count)])
        distance *= 2
    other = lax.ppermute(held, "shot", near)
    return jnp.where(odd == 0, jnp.concatenate([held, other]), jnp.concatenate([other, held]))


def local(wave_now, wave_prev, vel_coef, epsilon, delta, tilt, azimuth, aperture):
    second = lax.axis_index("gy")
    columns = lax.axis_size("gx")
    flags = jnp.stack([second.astype(jnp.int32), aperture[0, 0, 0].astype(jnp.int32)])
    model = jnp.stack([vel_coef, epsilon, delta, tilt.astype(F32), azimuth.astype(F32)])
    start = (1 - second) * (wave_now.shape[3] - TILE)
    rows = jnp.concatenate(
        [cut(wave_now[0], start, TILE, 2), cut(wave_prev[0], start, TILE, 2), cut(model, start, TILE, 2)]
    )
    border = lax.ppermute(rows, "gy", [(0, 1), (1, 0)])
    forward = [(i, i + 1) for i in range(columns - 1)]
    backward = [(i + 1, i) for i in range(columns - 1)]
    from_left = lax.ppermute(face(wave_now[0], wave_prev[0], model, False), "gx", forward)
    from_right = lax.ppermute(face(wave_now[0], wave_prev[0], model, True), "gx", backward)
    wave, edge_a, edge_b, edge_c, edge_corr, inside = advance_inner(
        flags, wave_now, wave_prev, vel_coef, epsilon, delta, tilt, azimuth, border
    )
    inside = sum_shots_halves(inside)
    halo = jnp.stack([from_left, from_right])
    corner = swap_y(halo, 2, second)
    wave, outside = advance_border(flags, edge_a, edge_b, edge_c, edge_corr, halo, corner, wave)
    outside = sum_shots(outside)
    return wave, jnp.concatenate([outside[0], inside, outside[1]])


def solution(mesh):
    return jax.shard_map(
        local,
        mesh=mesh,
        in_specs=(
            P("shot", None, "gx", "gy", None),
            P("shot", None, "gx", "gy", None),
            P("gx", "gy", None),
            P("gx", "gy", None),
            P("gx", "gy", None),
            P("gx", "gy", None),
            P("gx", "gy", None),
            P("shot", "gx", "gy"),
        ),
        out_specs=(P("shot", None, "gx", "gy", None), P("gx", "gy", None)),
        check_vma=False,
    )
```

```python
import functools
import math

import jax
import jax.numpy as jnp
from jax import lax
from jax.experimental import pallas as pl
from jax.experimental.pallas import tpu as pltpu
from jax.sharding import PartitionSpec as P

ITERS = 4
LANES = 128
TILE = 8
F32 = jnp.float32


def sin_cos(degrees):
    quadrant = jnp.floor(degrees * (1.0 / 90.0) + 0.5)
    angle = (degrees - 90.0 * quadrant) * (math.pi / 180.0)
    square = angle * angle
    sine = angle * (1.0 + square * (-1.0 / 6 + square * (1.0 / 120 + square * (-1.0 / 5040 + square * (1.0 / 362880)))))
    cosine = 1.0 + square * (
        -0.5 + square * (1.0 / 24 + square * (-1.0 / 720 + square * (1.0 / 40320 + square * (-1.0 / 3628800))))
    )
    turn = quadrant - 4.0 * jnp.floor(quadrant * 0.25)
    odd = (turn == 1.0) | (turn == 3.0)
    first = jnp.where(odd, cosine, sine)
    second = jnp.where(odd, sine, cosine)
    return (
        jnp.where(turn >= 2.0, -first, first),
        jnp.where((turn == 1.0) | (turn == 2.0), -second, second),
    )


def model_rows(vel, eps, delta, tilt, azimuth, mirrored):
    sin_t, cos_t = sin_cos(tilt)
    sin_a, cos_a = sin_cos(azimuth)
    nx, ny, nz = sin_t * cos_a, sin_t * sin_a, cos_t
    gain = 1.0 + 2.0 * eps
    root = jnp.sqrt(1.0 + 2.0 * delta)
    half_x = (-0.5 if mirrored else 0.5) * nx
    return (
        (nx * nx,) * 2,
        (ny * ny,) * 2,
        (half_x * ny,) * 2,
        (half_x * nz,) * 2,
        (0.5 * ny * nz,) * 2,
        (vel * gain, vel),
        (vel * root,) * 2,
    )


FACTORS = 7
SLOTS = 8
REACH = ITERS
CHUNKS = 2


def slot(half, field):
    return 4 * (field % 2) + 2 * half + field // 2


class Rows:
    def __init__(self, width_y, second):
        self.width_y = width_y
        self.total = width_y + REACH + 2
        self.own = 1 + REACH * second
        self.other = 1 + width_y * (1 - second)
        self.second = second

    def flat(self, plane, row, where, size):
        return pl.ds((plane * self.total + row) * SLOTS + where, size, stride=SLOTS)

    def tiles(self):
        return [slice(t, t + TILE) for t in range(0, self.width_y, TILE)]

    def pieces(self):
        return [(rows, TILE, self.own + rows.start) for rows in self.tiles()] + [(None, REACH, self.other)]


def z_terms(value, first_lane, last_lane):
    after = jnp.where(last_lane, 0.0, pltpu.roll(value, LANES - 1, 1))
    before = jnp.where(first_lane, 0.0, pltpu.roll(value, 1, 1))
    return after - before, after + before


def lane_ends(shape=(SLOTS, LANES)):
    lane = lax.broadcasted_iota(jnp.int32, shape, 1)
    return lane == 0, lane == LANES - 1


def sweep(old, new, slopes, sums, coef, planes, layout, step, done):
    count = layout.width_y + REACH - 1 - step
    first = 1 + (1 + step) * layout.second
    edges = lane_ends()
    is_q = lax.broadcasted_iota(jnp.int32, (SLOTS, LANES), 0) >= SLOTS // 2
    around = pl.ds(first - 1, count + 2)
    within = pl.ds(first, count)

    def plane(x):
        f_m, f_0, f_p = [old.at[x + i, around] for i in (-1, 0, 1)]
        g, h = slopes.at[pl.ds(x - 1, 3), around], sums.at[pl.ds(x, 2), around]
        out = new.at[x, within]
        factors = [coef.at[i, x, within] for i in range(FACTORS)]

        def column(j):
            below, above = f_m[j], f_p[j]
            g[2, j], h[1, j] = ahead = z_terms(above, *edges)
            return above - below, above + below, f_0[j], g[1, j], ahead[0]

        before, here = column(0), column(1)
        for j in range(count):
            after = column(j + 2)
            a, b, d, e, k, c1, c2 = [factor[j] for factor in factors]
            sum_z = h[0, j + 1]
            twice = here[2] + here[2]
            base = sum_z - twice
            over_x = here[1] - sum_z
            over_y = (after[2] + before[2]) - sum_z
            along = (
                (base + a * over_x)
                + (b * over_y + d * (after[0] - before[0]))
                + (e * (here[4] - g[0, j + 1]) + k * (after[3] - before[3]))
            )
            across = ((over_x + over_y) + 3.0 * base) - along
            mine = jnp.where(is_q, along, across)
            out[j] = (twice - out[j]) + (c1 * mine + c2 * pltpu.roll(mine, SLOTS // 2, 0))
            before, here = here, after
        done(x)

    for back in (1, 0):
        for j in range(count + 2):
            x, row = planes[0] - back, first - 1 + j
            slopes[x, row], sums[x, row] = z_terms(old[x, row], *edges)
    lax.fori_loop(*planes, lambda x, _: (plane(x), 0)[1], 0)


def seam(part, x, rows):
    low = lax.broadcasted_iota(jnp.int32, (SLOTS, LANES), 0) % 4 < 2
    for j in range(rows):
        value = part[x, j]
        part[x + 1, j] = jnp.where(low, pltpu.roll(value, SLOTS - 2, 0), pltpu.roll(value, 2, 0))


def clear_ends(refs, rows):
    for ref in refs:
        empty = jnp.zeros((ref.shape[0], 1) + ref.shape[2:], F32)
        ref[:, 0:1] = empty
        ref[:, rows - 1 : rows] = empty


def copies(pairs, sems, base=0):
    out = []
    for i, (source, target) in enumerate(pairs):
        out.append(pltpu.make_async_copy(source, target, sems.at[base + i]))
        out[-1].start()
    return out


def flat_view(ref):
    size = 1
    for length in ref.shape[:-1]:
        size *= length
    return ref.reshape(size, ref.shape[-1])


def put_model(coef, layout, plane, half, row, size, raw):
    parts = model_rows(*raw, half == 1)
    for i, both in enumerate(parts):
        flat = flat_view(coef.at[i])
        for field in range(4):
            flat[layout.flat(plane, row, slot(half, field), size), :] = both[field % 2]


def products(flat, layout, plane, half, rows):
    where = [layout.flat(plane, layout.own + rows.start, slot(half, field), TILE) for field in (0, 2)]
    return flat[where[0], :] * flat[where[1], :]


def inner_kernel(
    cover, now, prev, vel, eps, delta, tilt, azimuth, border,
    wave, edge_a, edge_b, edge_c, edge_corr, kept, sent,
    fa, fb, slopes, sums, coef, corr, in_now, in_prev, raw, raw_int, in_border, load_sems, sems, wave_sems,
):
    second, odd = lax.axis_index("gy"), lax.axis_index("shot") % 2
    width_x, width_y = vel.shape[0], vel.shape[1]
    half_x = width_x // 2
    layout = Rows(width_y, second)
    rows = layout.total
    chunk = half_x // CHUNKS
    loads = []
    for c in range(CHUNKS):
        pairs = [(border, in_border)] if c == 0 else []
        for start in (c * chunk, width_x - (c + 1) * chunk):
            at = pl.ds(start, chunk)
            pairs += [(now.at[0, :, at], in_now.at[:, at]), (prev.at[0, :, at], in_prev.at[:, at])]
            pairs += [(array.at[at], raw.at[n, at]) for n, array in enumerate((vel, eps, delta))]
            pairs += [(array.at[at], raw_int.at[n, at]) for n, array in enumerate((tilt, azimuth))]
        loads.append(copies(pairs, load_sems.at[c]))
    clear_ends((fa, fb), rows)

    def fill(i, _):
        for half in range(2):
            x = i if half == 0 else width_x - 1 - i
            for field in range(4):
                for own, size, row in layout.pieces():
                    spot = layout.flat(i, row, slot(half, field), size)
                    if own is None:
                        flat_view(fa)[spot, :] = in_border[field, x]
                        flat_view(fb)[spot, :] = in_border[4 + field, x]
                    else:
                        flat_view(fa)[spot, :] = in_now[field, x, own, :]
                        flat_view(fb)[spot, :] = in_prev[field, x, own, :]
        for half in range(2):
            x = i if half == 0 else width_x - 1 - i
            for own, size, row in layout.pieces():
                if own is None:
                    cells = [in_border[8 + n, x] for n in range(5)]
                else:
                    cells = [raw[n, x, own, :] for n in range(3)]
                    cells += [raw_int[n, x, own, :].astype(F32) for n in range(2)]
                put_model(coef, layout, i, half, row, size, cells)
        return 0

    for c in range(CHUNKS):
        for copy in loads[c]:
            copy.wait()
        lax.fori_loop(c * chunk, (c + 1) * chunk, fill, 0)
    out = copies([(coef.at[:, pl.ds(0, ITERS)], edge_c)], sems, 9)
    seam(fa, half_x - 1, rows)
    bufs = (fa, fb)
    scale = cover[0, 0, 0].astype(F32) / ITERS

    def give_wave(i, half):
        x = i if half == 0 else width_x - 1 - i
        return pltpu.make_async_copy(in_now.at[:, x], wave.at[0, :, x], wave_sems.at[half * half_x + i])

    def finished(step):
        flat = flat_view(bufs[1 - step % 2])

        def done(i):
            for half in range(2):
                x = i if half == 0 else width_x - 1 - i
                for own in layout.tiles():
                    product = products(flat, layout, i, half, own)
                    total = product if step == 0 else corr[x, own, :] + product
                    corr[x, own, :] = scale * total if step == ITERS - 1 else total
                    if step == ITERS - 1:
                        for field in range(4):
                            spot = layout.flat(i, layout.own + own.start, slot(half, field), TILE)
                            in_now[field, x, own, :] = flat[spot, :]
                if step == ITERS - 1:
                    give_wave(i, half).start()

        return done

    for step in range(ITERS):
        old, new = bufs[step % 2], bufs[1 - step % 2]
        sweep(old, new, slopes, sums, coef, (1 + step, half_x), layout, step, finished(step))
        if step < ITERS - 1:
            seam(new, half_x - 1, rows)
        if step == ITERS - 3:
            out += copies([(fa.at[pl.ds(0, ITERS)], edge_a)], sems, 10)
        if step == ITERS - 2:
            far = pl.ds(width_x - ITERS, ITERS)
            out += copies(
                [
                    (fb.at[pl.ds(0, ITERS + 1)], edge_b),
                    (corr.at[pl.ds(0, ITERS)], edge_corr.at[0]),
                    (corr.at[far], edge_corr.at[1]),
                ],
                sems,
                11,
            )
    part = half_x - ITERS
    out += copies(
        [
            (corr.at[pl.ds(ITERS + part * odd, part)], kept),
            (corr.at[pl.ds(ITERS + part * (1 - odd), part)], sent),
        ],
        sems,
        14,
    )
    for copy in out:
        copy.wait()
    for i in range(ITERS, half_x):
        for half in range(2):
            give_wave(i, half).wait()


def border_kernel(
    cover, edge_a, edge_b, edge_c, edge_corr, near, far, corner, wave_in,
    wave, image,
    fa, fb, slopes, sums, coef, corr, sides, corners, in_now, sems,
):
    second, odd = lax.axis_index("gy"), lax.axis_index("gx") % 2
    width_x, width_y = wave.shape[2], wave.shape[3]
    layout = Rows(width_y, second)
    rows = layout.total
    loads = copies(
        [
            (near, sides.at[1 - odd]),
            (far, sides.at[odd]),
            (corner.at[0], corners.at[1 - odd]),
            (corner.at[1], corners.at[odd]),
            (edge_a, fa.at[pl.ds(ITERS, ITERS)]),
            (edge_b, fb.at[pl.ds(ITERS, ITERS + 1)]),
            (edge_corr, corr),
            (edge_c, coef.at[:, pl.ds(ITERS, ITERS)]),
        ],
        sems,
    )
    clear_ends([ref.at[pl.ds(0, ITERS)] for ref in (fa, fb)], rows)
    for copy in loads[:4]:
        copy.wait()
    n_now, n_prev, less = 4 * ITERS, 4 * (ITERS - 1), ITERS - 1

    def cells(half, index, own):
        return corners[half, index] if own is None else sides[half, index, own, :]

    def fill(j, _):
        for half in range(2):
            natural = j if half == 0 else ITERS - 1 - j
            shorter = jnp.maximum(j - 1, 0) if half == 0 else jnp.minimum(ITERS - 1 - j, less - 1)
            for own, size, row in layout.pieces():
                for field in range(4):
                    spot = layout.flat(j, row, slot(half, field), size)
                    flat_view(fa)[spot, :] = cells(half, field * ITERS + natural, own)
                    flat_view(fb)[spot, :] = cells(half, n_now + field * less + shorter, own)
        for half in range(2):
            shorter = jnp.maximum(j - 1, 0) if half == 0 else jnp.minimum(ITERS - 1 - j, less - 1)
            for own, size, row in layout.pieces():
                raw = [cells(half, n_now + n_prev + n * less + shorter, own) for n in range(5)]
                put_model(coef, layout, j, half, row, size, raw)
        return 0

    lax.fori_loop(0, ITERS, fill, 0)
    for copy in loads[4:]:
        copy.wait()

    corr[0, 0] = jnp.zeros(corr.shape[2:], F32)
    corr[1, ITERS - 1] = jnp.zeros(corr.shape[2:], F32)

    def finished(flat):
        def done(i):
            @pl.when(i >= ITERS)
            def _():
                for half in range(2):
                    x = i - ITERS if half == 0 else 2 * ITERS - 1 - i
                    for own in layout.tiles():
                        corr[half, x, own, :] = corr[half, x, own, :] + products(flat, layout, i, half, own)

        return done

    def advance(turn, _):
        for step, (old, new) in enumerate(((fa, fb), (fb, fa))):
            start = 1 + step + 2 * turn
            sweep(old, new, slopes, sums, coef, (start, start + ITERS), layout, 0, finished(flat_view(new)))
        return 0

    lax.fori_loop(0, ITERS // 2, advance, 0)
    scale = cover[0, 0, 0].astype(F32) / ITERS
    corr[...] = scale * corr[...]
    out = copies([(corr, image)], sems)
    flat = flat_view(fa)

    def give(i, _):
        for half in range(2):
            x = i if half == 0 else ITERS - 1 - i
            for own in layout.tiles():
                for field in range(4):
                    spot = layout.flat(ITERS + i, layout.own + own.start, slot(half, field), TILE)
                    in_now[half, field, x, own, :] = flat[spot, :]
        return 0

    lax.fori_loop(0, ITERS, give, 0)
    out += copies(
        [
            (in_now.at[0], wave.at[0, :, pl.ds(0, ITERS)]),
            (in_now.at[1], wave.at[0, :, pl.ds(width_x - ITERS, ITERS)]),
        ],
        sems,
        1,
    )
    for copy in out:
        copy.wait()


def any_specs(count):
    return [pl.BlockSpec(memory_space=pl.ANY)] * count


MIB = 1024 * 1024


def pack_kernel(
    now, prev, vel, eps, delta, tilt, azimuth,
    near, far, border,
    planes_int, wave_rows, float_rows, int_rows, sems,
):
    second, odd = lax.axis_index("gy"), lax.axis_index("gx") % 2
    width_x, width_y = vel.shape[0], vel.shape[1]
    deep, less = ITERS, ITERS - 1
    n_now, n_prev = 4 * deep, 4 * less
    ints, floats = (tilt, azimuth), (vel, eps, delta)
    tile = pl.ds(pl.multiple_of((1 - second) * (width_y - TILE), TILE), TILE)
    pairs = [(array.at[0, :, :, tile], wave_rows.at[n]) for n, array in enumerate((now, prev))]
    pairs += [(array.at[:, tile], float_rows.at[n]) for n, array in enumerate(floats)]
    pairs += [(array.at[:, tile], int_rows.at[n]) for n, array in enumerate(ints)]
    ends = ((near, 1 - odd), (far, odd))
    for k, (_, high) in enumerate(ends):
        at = pl.ds(high * (width_x - less), less)
        pairs += [(ints[n].at[at], planes_int.at[k, n]) for n in range(2)]
    first = len(pairs)
    for out, high in ends:
        at = pl.ds(high * (width_x - less), less)
        for f in range(4):
            pairs.append((now.at[0, f, pl.ds(high * (width_x - deep), deep)], out.at[pl.ds(f * deep, deep)]))
            pairs.append((prev.at[0, f, at], out.at[pl.ds(n_now + f * less, less)]))
        for n in range(3):
            pairs.append((floats[n].at[at], out.at[pl.ds(n_now + n_prev + n * less, less)]))
    started = copies(pairs, sems)
    for copy in started[:first]:
        copy.wait()
    for k, (out, _) in enumerate(ends):
        for n in range(2):
            begin = n_now + n_prev + (3 + n) * less
            out[begin : begin + less] = planes_int[k, n].astype(F32)

    def needed(ref, *spot):
        return jnp.where(second == 1, ref[spot + (slice(0, REACH),)], ref[spot + (slice(TILE - REACH, TILE),)])

    def rows(x, _):
        for kind in range(2):
            for f in range(4):
                border[4 * kind + f, x] = needed(wave_rows, kind, f, x)
        for n in range(3):
            border[8 + n, x] = needed(float_rows, n, x)
        for n in range(2):
            border[11 + n, x] = needed(int_rows, n, x).astype(F32)
        return 0

    lax.fori_loop(0, width_x, rows, 0)
    for copy in started[first:]:
        copy.wait()


def pack(now, prev, vel, eps, delta, tilt, azimuth):
    width_x, width_y = vel.shape[0], vel.shape[1]
    planes = 4 * ITERS + 9 * (ITERS - 1)
    face = jax.ShapeDtypeStruct((planes, width_y, LANES), F32)
    return pl.pallas_call(
        pack_kernel,
        in_specs=any_specs(7),
        out_specs=[pl.BlockSpec(memory_space=pltpu.VMEM)] * 3,
        out_shape=(face, face, jax.ShapeDtypeStruct((13, width_x, REACH, LANES), F32)),
        scratch_shapes=[
            pltpu.VMEM((2, 2, ITERS - 1, width_y, LANES), jnp.int32),
            pltpu.VMEM((2, 4, width_x, TILE, LANES), F32),
            pltpu.VMEM((3, width_x, TILE, LANES), F32),
            pltpu.VMEM((2, width_x, TILE, LANES), jnp.int32),
            pltpu.SemaphoreType.DMA((33,)),
        ],
        compiler_params=pltpu.CompilerParams(vmem_limit_bytes=60 * MIB),
        cost_estimate=pl.CostEstimate(flops=1_000_000, bytes_accessed=8_000_000, transcendentals=0),
        name="pack_borders",
    )(now, prev, vel, eps, delta, tilt, azimuth)


def advance_inner(cover, now, prev, vel, eps, delta, tilt, azimuth, border):
    width_x, width_y = vel.shape[0], vel.shape[1]
    rows = width_y + REACH + 2
    half_x = width_x // 2
    shape = functools.partial(jax.ShapeDtypeStruct, dtype=F32)
    block = (half_x + 1, rows, SLOTS, LANES)
    part = shape((half_x - ITERS, width_y, LANES))
    vmem = lambda size: pltpu.VMEM(size, F32)
    return pl.pallas_call(
        inner_kernel,
        in_specs=[pl.BlockSpec(memory_space=pltpu.SMEM)] + any_specs(8),
        out_specs=any_specs(7),
        out_shape=(
            shape(now.shape),
            shape((ITERS,) + block[1:]),
            shape((ITERS + 1,) + block[1:]),
            shape((FACTORS, ITERS) + block[1:]),
            shape((2, ITERS, width_y, LANES)),
            part,
            part,
        ),
        scratch_shapes=[vmem(block)] * 4
        + [
            vmem((FACTORS, half_x) + block[1:]),
            vmem(vel.shape),
            vmem(now.shape[1:]),
            vmem(now.shape[1:]),
            vmem((3, width_x, width_y, LANES)),
            pltpu.VMEM((2, width_x, width_y, LANES), jnp.int32),
            vmem(border.shape),
            pltpu.SemaphoreType.DMA((CHUNKS, 15)),
            pltpu.SemaphoreType.DMA((16,)),
            pltpu.SemaphoreType.DMA((width_x,)),
        ],
        compiler_params=pltpu.CompilerParams(vmem_limit_bytes=60 * MIB),
        cost_estimate=pl.CostEstimate(flops=80_000_000, bytes_accessed=200_000_000, transcendentals=0),
        name="inner_steps",
    )(cover, now, prev, vel, eps, delta, tilt, azimuth, border)


def advance_border(cover, edge_a, edge_b, edge_c, edge_corr, near, far, corner, wave):
    width_y = wave.shape[3]
    rows = width_y + REACH + 2
    block = (2 * ITERS + 1, rows, SLOTS, LANES)
    shape = functools.partial(jax.ShapeDtypeStruct, dtype=F32)
    vmem = lambda size: pltpu.VMEM(size, F32)
    return pl.pallas_call(
        border_kernel,
        in_specs=[pl.BlockSpec(memory_space=pltpu.SMEM)] + any_specs(8),
        out_specs=any_specs(2),
        out_shape=(shape(wave.shape), shape(edge_corr.shape)),
        scratch_shapes=[vmem(block)] * 4
        + [
            vmem((FACTORS,) + block),
            vmem(edge_corr.shape),
            vmem((2,) + near.shape),
            vmem(corner.shape),
            vmem((2, 4, ITERS, width_y, LANES)),
            pltpu.SemaphoreType.DMA((8,)),
        ],
        input_output_aliases={8: 0},
        compiler_params=pltpu.CompilerParams(vmem_limit_bytes=60 * MIB),
        cost_estimate=pl.CostEstimate(flops=20_000_000, bytes_accessed=20_000_000, transcendentals=0),
        name="border_steps",
    )(cover, edge_a, edge_b, edge_c, edge_corr, near, far, corner, wave)


def cut(array, start, size, axis):
    return lax.dynamic_slice_in_dim(array, start, size, axis=axis)


def other_rows(block, axis, second):
    return cut(block, (1 - second) * (block.shape[axis] - REACH), REACH, axis)


def swap_cores(rows):
    return lax.ppermute(rows, "gy", [(0, 1), (1, 0)])


def pairs_at(distance):
    return [(i, i ^ distance) for i in range(lax.axis_size("shot"))]


def local(wave_now, wave_prev, vel_coef, epsilon, delta, tilt, azimuth, aperture):
    second = lax.axis_index("gy")
    columns = lax.axis_size("gx")
    inputs = (wave_now, wave_prev, vel_coef, epsilon, delta, tilt, azimuth)
    near, far, border = pack(*inputs)
    far = lax.ppermute(far, "gx", [(i, j) for i in range(1, columns - 1) for j in [i + 1 if i % 2 else i - 1]])
    near = lax.ppermute(near, "gx", [(i, i ^ 1) for i in range(columns) if i ^ 1 < columns])
    border = swap_cores(border)
    wave, edge_a, edge_b, edge_c, edge_corr, kept, sent = advance_inner(aperture, *inputs, border)
    kept, near, far = lax.optimization_barrier((kept, near, far))
    held = kept + lax.ppermute(sent, "shot", pairs_at(1))
    corner = swap_cores(jnp.stack([other_rows(f, 1, second) for f in (near, far)]))
    held, edge_corr = lax.optimization_barrier((held, edge_corr))
    wave, outside = advance_border(aperture, edge_a, edge_b, edge_c, edge_corr, near, far, corner, wave)
    distance = 2
    while distance < lax.axis_size("shot"):
        held = held + lax.ppermute(held, "shot", pairs_at(distance))
        distance *= 2
    held, outside = lax.optimization_barrier((held, outside))
    distance = 1
    while distance < lax.axis_size("shot"):
        outside = outside + lax.ppermute(outside, "shot", pairs_at(distance))
        if distance == 1:
            held, outside = lax.optimization_barrier((held, outside))
            other = lax.ppermute(held, "shot", pairs_at(1))
        distance *= 2
    even = lax.axis_index("shot") % 2 == 0
    first, then = jnp.where(even, held, other), jnp.where(even, other, held)
    return wave, jnp.concatenate([outside[0], first, then, outside[1]])


def solution(mesh):
    return jax.shard_map(
        local,
        mesh=mesh,
        in_specs=(
            P("shot", None, "gx", "gy", None),
            P("shot", None, "gx", "gy", None),
            P("gx", "gy", None),
            P("gx", "gy", None),
            P("gx", "gy", None),
            P("gx", "gy", None),
            P("gx", "gy", None),
            P("shot", "gx", "gy"),
        ),
        out_specs=(P("shot", None, "gx", "gy", None), P("gx", "gy", None)),
        check_vma=False,
    )
```

```python
import functools
import math

import jax
import jax.numpy as jnp
from jax import lax
from jax.experimental import pallas as pl
from jax.experimental.pallas import tpu as pltpu
from jax.sharding import PartitionSpec as P

ITERS = 4
LANES = 128
TILE = 8
F32 = jnp.float32


def polynomial(square, start, terms):
    factors = [1.0]
    for k in range(start, start + 2 * terms, 2):
        factors.append(-factors[-1] / ((k + 1) * (k + 2)))
    result = factors[-1]
    for factor in factors[-2::-1]:
        result = factor + square * result
    return result


def sin_cos_near(degrees, terms):
    angle = degrees * (math.pi / 180.0)
    square = angle * angle
    return angle * polynomial(square, 1, terms), polynomial(square, 0, terms + 1)


def sin_cos(degrees):
    quadrant = jnp.floor(degrees * (1.0 / 90.0) + 0.5)
    sine, cosine = sin_cos_near(degrees - 90.0 * quadrant, 4)
    odd = (quadrant == 1.0) | (quadrant == 3.0)
    first = jnp.where(odd, cosine, sine)
    second = jnp.where(odd, sine, cosine)
    back = (quadrant == 2.0) | (quadrant == 3.0)
    left = (quadrant == 1.0) | (quadrant == 2.0)
    return jnp.where(back, -first, first), jnp.where(left, -second, second)


def model_rows(vel, eps, delta, tilt, azimuth, mirrored):
    sin_t, cos_t = sin_cos_near(tilt, 6)
    sin_a, cos_a = sin_cos(azimuth)
    nx, ny, nz = sin_t * cos_a, sin_t * sin_a, cos_t
    gain = 1.0 + 2.0 * eps
    root = jnp.sqrt(1.0 + 2.0 * delta)
    half_x = (-0.5 if mirrored else 0.5) * nx
    return nx * nx, ny * ny, half_x * ny, half_x * nz, 0.5 * ny * nz, vel * gain, vel, vel * root


FACTORS = 7
SLOTS = 8
REACH = ITERS
CHUNKS = 4


def slot(half, field):
    return 4 * (field % 2) + 2 * half + field // 2


class Rows:
    def __init__(self, width_y, second):
        self.width_y = width_y
        self.total = width_y + REACH + 2
        self.own = 1 + REACH * second
        self.other = 1 + width_y * (1 - second)
        self.second = second

    def flat(self, plane, row, where, size):
        return pl.ds((plane * self.total + row) * SLOTS + where, size, stride=SLOTS)

    def tiles(self):
        return [slice(t, t + TILE) for t in range(0, self.width_y, TILE)]

    def pieces(self):
        return [(rows, TILE, self.own + rows.start) for rows in self.tiles()] + [(None, REACH, self.other)]


def z_terms(value, first_lane, last_lane):
    after = jnp.where(last_lane, 0.0, pltpu.roll(value, LANES - 1, 1))
    before = jnp.where(first_lane, 0.0, pltpu.roll(value, 1, 1))
    return after - before, after + before


def lane_ends(shape=(SLOTS, LANES)):
    lane = lax.broadcasted_iota(jnp.int32, shape, 1)
    return lane == 0, lane == LANES - 1


def sweep(old, new, slopes, sums, coef, planes, layout, step, done):
    count = layout.width_y + REACH - 1 - step
    first = 1 + (1 + step) * layout.second
    edges = lane_ends()
    is_q = lax.broadcasted_iota(jnp.int32, (SLOTS, LANES), 0) >= SLOTS // 2
    around = pl.ds(first - 1, count + 2)
    within = pl.ds(first, count)

    def plane(x):
        f_m, f_0, f_p = [old.at[x + i, around] for i in (-1, 0, 1)]
        g, h = slopes.at[pl.ds(x - 1, 3), around], sums.at[pl.ds(x, 2), around]
        out = new.at[x, within]
        factors = [coef.at[i, x, within] for i in range(FACTORS)]

        def column(j):
            below, above = f_m[j], f_p[j]
            g[2, j], h[1, j] = ahead = z_terms(above, *edges)
            return above - below, above + below, f_0[j], g[1, j], ahead[0]

        before, here = column(0), column(1)
        for j in range(count):
            after = column(j + 2)
            a, b, d, e, k, c1, c2 = [factor[j] for factor in factors]
            sum_z = h[0, j + 1]
            twice = here[2] + here[2]
            base = sum_z - twice
            over_x = here[1] - sum_z
            over_y = (after[2] + before[2]) - sum_z
            along = (
                (base + a * over_x)
                + (b * over_y + d * (after[0] - before[0]))
                + (e * (here[4] - g[0, j + 1]) + k * (after[3] - before[3]))
            )
            across = ((over_x + over_y) + 3.0 * base) - along
            mine = jnp.where(is_q, along, across)
            out[j] = (twice - out[j]) + (c1 * mine + c2 * pltpu.roll(mine, SLOTS // 2, 0))
            before, here = here, after
        done(x)

    for back in (1, 0):
        for j in range(count + 2):
            x, row = planes[0] - back, first - 1 + j
            slopes[x, row], sums[x, row] = z_terms(old[x, row], *edges)
    lax.fori_loop(*planes, lambda x, _: (plane(x), 0)[1], 0)


def seam(part, x, rows):
    low = lax.broadcasted_iota(jnp.int32, (SLOTS, LANES), 0) % 4 < 2
    for j in range(rows):
        value = part[x, j]
        part[x + 1, j] = jnp.where(low, pltpu.roll(value, SLOTS - 2, 0), pltpu.roll(value, 2, 0))


def clear_ends(refs, rows):
    for ref in refs:
        empty = jnp.zeros((ref.shape[0], 1) + ref.shape[2:], F32)
        ref[:, 0:1] = empty
        ref[:, rows - 1 : rows] = empty


def copies(pairs, sems, base=0):
    out = []
    for i, (source, target) in enumerate(pairs):
        out.append(pltpu.make_async_copy(source, target, sems.at[base + i]))
        out[-1].start()
    return out


def flat_view(ref):
    size = 1
    for length in ref.shape[:-1]:
        size *= length
    return ref.reshape(size, ref.shape[-1])


def put_model(natural, half, row, size, raw):
    for i, part in enumerate(model_rows(*raw, half == 1)):
        natural[half, i, row : row + size, :] = part


def spread_model(coef, natural, plane, layout):
    sublane = lax.broadcasted_iota(jnp.int32, (SLOTS, LANES), 0)
    is_q, is_mirrored = sublane >= SLOTS // 2, sublane % 4 >= 2

    def cell(i, row):
        low, high = [natural[half, i, pl.ds(row, SLOTS, stride=0), :] for half in range(2)]
        return jnp.where(is_mirrored, high, low)

    for begin, first, size in ((0, layout.own, layout.width_y), (layout.width_y, layout.other, REACH)):
        out = coef.at[:, plane, pl.ds(first, size)]
        for j in range(size):
            for i in range(5):
                out[i, j] = cell(i, begin + j)
            out[5, j] = jnp.where(is_q, cell(6, begin + j), cell(5, begin + j))
            out[6, j] = cell(7, begin + j)


def products(flat, layout, plane, half, rows):
    where = [layout.flat(plane, layout.own + rows.start, slot(half, field), TILE) for field in (0, 2)]
    return flat[where[0], :] * flat[where[1], :]


def inner_kernel(
    cover, now, prev, vel, eps, delta, tilt, azimuth, border,
    wave, edge_a, edge_b, edge_c, edge_corr, kept, sent,
    fa, fb, slopes, sums, coef, corr, in_now, in_prev, raw, raw_int, in_border, natural, load_sems, sems, wave_sems,
):
    second, odd = lax.axis_index("gy"), lax.axis_index("shot") % 2
    width_x, width_y = vel.shape[0], vel.shape[1]
    half_x = width_x // 2
    layout = Rows(width_y, second)
    rows = layout.total
    chunk = half_x // CHUNKS
    loads = []
    for c in range(CHUNKS):
        pairs = [(border, in_border)] if c == 0 else []
        for start in (c * chunk, width_x - (c + 1) * chunk):
            at = pl.ds(start, chunk)
            pairs += [(now.at[0, :, at], in_now.at[:, at]), (prev.at[0, :, at], in_prev.at[:, at])]
            pairs += [(array.at[at], raw.at[n, at]) for n, array in enumerate((vel, eps, delta))]
            pairs += [(array.at[at], raw_int.at[n, at]) for n, array in enumerate((tilt, azimuth))]
        loads.append(copies(pairs, load_sems.at[c]))
    clear_ends((fa, fb), rows)

    def fill(i, _):
        for half in range(2):
            x = i if half == 0 else width_x - 1 - i
            for field in range(4):
                for own, size, row in layout.pieces():
                    spot = layout.flat(i, row, slot(half, field), size)
                    if own is None:
                        flat_view(fa)[spot, :] = in_border[field, x]
                        flat_view(fb)[spot, :] = in_border[4 + field, x]
                    else:
                        flat_view(fa)[spot, :] = in_now[field, x, own, :]
                        flat_view(fb)[spot, :] = in_prev[field, x, own, :]
        for half in range(2):
            x = i if half == 0 else width_x - 1 - i
            for own, size, row in layout.pieces():
                if own is None:
                    cells = [in_border[8 + n, x] for n in range(5)]
                else:
                    cells = [raw[n, x, own, :] for n in range(3)]
                    cells += [raw_int[n, x, own, :].astype(F32) for n in range(2)]
                put_model(natural, half, own.start if own else width_y, size, cells)
        spread_model(coef, natural, i, layout)
        return 0

    for c in range(CHUNKS):
        for copy in loads[c]:
            copy.wait()
        lax.fori_loop(c * chunk, (c + 1) * chunk, fill, 0)
    out = copies([(coef.at[:, pl.ds(0, ITERS)], edge_c)], sems, 9)
    seam(fa, half_x - 1, rows)
    bufs = (fa, fb)
    covered = cover[0, 0, 0].astype(F32)
    scales = [jnp.where(odd == half, covered, covered / ITERS) for half in range(2)]

    def give_wave(i, half):
        x = i if half == 0 else width_x - 1 - i
        return pltpu.make_async_copy(in_now.at[:, x], wave.at[0, :, x], wave_sems.at[half * half_x + i])

    def finished(step):
        flat = flat_view(bufs[1 - step % 2])

        def done(i):
            for half in range(2):
                x = i if half == 0 else width_x - 1 - i
                for own in layout.tiles():
                    product = products(flat, layout, i, half, own)
                    total = product if step == 0 else corr[x, own, :] + product
                    corr[x, own, :] = scales[half] * total if step == ITERS - 1 else total
                    if step == ITERS - 1:
                        for field in range(4):
                            spot = layout.flat(i, layout.own + own.start, slot(half, field), TILE)
                            in_now[field, x, own, :] = flat[spot, :]
                if step == ITERS - 1:
                    give_wave(i, half).start()

        return done

    for step in range(ITERS):
        old, new = bufs[step % 2], bufs[1 - step % 2]
        sweep(old, new, slopes, sums, coef, (1 + step, half_x), layout, step, finished(step))
        if step < ITERS - 1:
            seam(new, half_x - 1, rows)
        if step == ITERS - 3:
            out += copies([(fa.at[pl.ds(0, ITERS)], edge_a)], sems, 10)
        if step == ITERS - 2:
            far = pl.ds(width_x - ITERS, ITERS)
            out += copies(
                [
                    (fb.at[pl.ds(0, ITERS + 1)], edge_b),
                    (corr.at[pl.ds(0, ITERS)], edge_corr.at[0]),
                    (corr.at[far], edge_corr.at[1]),
                ],
                sems,
                11,
            )
    part = half_x - ITERS
    out += copies(
        [
            (corr.at[pl.ds(ITERS + part * odd, part)], kept),
            (corr.at[pl.ds(ITERS + part * (1 - odd), part)], sent),
        ],
        sems,
        14,
    )
    for copy in out:
        copy.wait()
    for i in range(ITERS, half_x):
        for half in range(2):
            give_wave(i, half).wait()


def border_kernel(
    cover, edge_a, edge_b, edge_c, edge_corr, near, far, corner, wave_in,
    wave, image, image_own,
    fa, fb, slopes, sums, coef, corr, sides, corners, natural, in_now, picture, sems,
):
    second, odd = lax.axis_index("gy"), lax.axis_index("gx") % 2
    width_x, width_y = wave.shape[2], wave.shape[3]
    layout = Rows(width_y, second)
    rows = layout.total
    loads = copies(
        [
            (near, sides.at[1 - odd]),
            (far, sides.at[odd]),
            (corner.at[0], corners.at[1 - odd]),
            (corner.at[1], corners.at[odd]),
            (edge_a, fa.at[pl.ds(ITERS, ITERS)]),
            (edge_b, fb.at[pl.ds(ITERS, ITERS + 1)]),
            (edge_corr, corr),
            (edge_c, coef.at[:, pl.ds(ITERS, ITERS)]),
        ],
        sems,
    )
    clear_ends([ref.at[pl.ds(0, ITERS)] for ref in (fa, fb)], rows)
    for copy in loads[:4]:
        copy.wait()
    n_now, n_prev, less = 4 * ITERS, 4 * (ITERS - 1), ITERS - 1

    def cells(half, index, own):
        return corners[half, index] if own is None else sides[half, index, own, :]

    def fill(j, _):
        for half in range(2):
            nth = j if half == 0 else ITERS - 1 - j
            shorter = jnp.maximum(j - 1, 0) if half == 0 else jnp.minimum(ITERS - 1 - j, less - 1)
            for own, size, row in layout.pieces():
                for field in range(4):
                    spot = layout.flat(j, row, slot(half, field), size)
                    flat_view(fa)[spot, :] = cells(half, field * ITERS + nth, own)
                    flat_view(fb)[spot, :] = cells(half, n_now + field * less + shorter, own)
        for half in range(2):
            shorter = jnp.maximum(j - 1, 0) if half == 0 else jnp.minimum(ITERS - 1 - j, less - 1)
            for own, size, row in layout.pieces():
                raw = [cells(half, n_now + n_prev + n * less + shorter, own) for n in range(5)]
                put_model(natural, half, own.start if own else width_y, size, raw)
        spread_model(coef, natural, j, layout)
        return 0

    lax.fori_loop(0, ITERS, fill, 0)
    for copy in loads[4:]:
        copy.wait()

    corr[0, 0] = jnp.zeros(corr.shape[2:], F32)
    corr[1, ITERS - 1] = jnp.zeros(corr.shape[2:], F32)

    def finished(flat):
        def done(i):
            @pl.when(i >= ITERS)
            def _():
                for half in range(2):
                    x = i - ITERS if half == 0 else 2 * ITERS - 1 - i
                    for own in layout.tiles():
                        corr[half, x, own, :] = corr[half, x, own, :] + products(flat, layout, i, half, own)

        return done

    def advance(turn, _):
        for step, (old, new) in enumerate(((fa, fb), (fb, fa))):
            start = 1 + step + 2 * turn
            sweep(old, new, slopes, sums, coef, (start, start + ITERS), layout, 0, finished(flat_view(new)))
        return 0

    lax.fori_loop(0, ITERS // 2, advance, 0)
    corr[...] = cover[0, 0, 0].astype(F32) * corr[...]
    picture[...] = corr[...] * (1.0 / ITERS)
    out = copies([(picture, image), (corr, image_own)], sems)
    flat = flat_view(fa)

    def give(i, _):
        for half in range(2):
            x = i if half == 0 else ITERS - 1 - i
            for own in layout.tiles():
                for field in range(4):
                    spot = layout.flat(ITERS + i, layout.own + own.start, slot(half, field), TILE)
                    in_now[half, field, x, own, :] = flat[spot, :]
        return 0

    lax.fori_loop(0, ITERS, give, 0)
    out += copies(
        [
            (in_now.at[0], wave.at[0, :, pl.ds(0, ITERS)]),
            (in_now.at[1], wave.at[0, :, pl.ds(width_x - ITERS, ITERS)]),
        ],
        sems,
        2,
    )
    for copy in out:
        copy.wait()


def any_specs(count):
    return [pl.BlockSpec(memory_space=pl.ANY)] * count


MIB = 1024 * 1024


def pack_kernel(
    now, prev, vel, eps, delta, tilt, azimuth,
    near, far, border,
    planes_int, wave_rows, float_rows, int_rows, sems,
):
    second, odd = lax.axis_index("gy"), lax.axis_index("gx") % 2
    width_x, width_y = vel.shape[0], vel.shape[1]
    deep, less = ITERS, ITERS - 1
    n_now, n_prev = 4 * deep, 4 * less
    ints, floats = (tilt, azimuth), (vel, eps, delta)
    tile = pl.ds(pl.multiple_of((1 - second) * (width_y - TILE), TILE), TILE)
    pairs = [(array.at[0, :, :, tile], wave_rows.at[n]) for n, array in enumerate((now, prev))]
    pairs += [(array.at[:, tile], float_rows.at[n]) for n, array in enumerate(floats)]
    pairs += [(array.at[:, tile], int_rows.at[n]) for n, array in enumerate(ints)]
    ends = ((near, 1 - odd), (far, odd))
    for k, (_, high) in enumerate(ends):
        at = pl.ds(high * (width_x - less), less)
        pairs += [(ints[n].at[at], planes_int.at[k, n]) for n in range(2)]
    first = len(pairs)
    for out, high in ends:
        at = pl.ds(high * (width_x - less), less)
        for f in range(4):
            pairs.append((now.at[0, f, pl.ds(high * (width_x - deep), deep)], out.at[pl.ds(f * deep, deep)]))
            pairs.append((prev.at[0, f, at], out.at[pl.ds(n_now + f * less, less)]))
        for n in range(3):
            pairs.append((floats[n].at[at], out.at[pl.ds(n_now + n_prev + n * less, less)]))
    started = copies(pairs, sems)
    for copy in started[:first]:
        copy.wait()
    for k, (out, _) in enumerate(ends):
        for n in range(2):
            begin = n_now + n_prev + (3 + n) * less
            out[begin : begin + less] = planes_int[k, n].astype(F32)

    def needed(ref, *spot):
        return jnp.where(second == 1, ref[spot + (slice(0, REACH),)], ref[spot + (slice(TILE - REACH, TILE),)])

    def rows(x, _):
        for kind in range(2):
            for f in range(4):
                border[4 * kind + f, x] = needed(wave_rows, kind, f, x)
        for n in range(3):
            border[8 + n, x] = needed(float_rows, n, x)
        for n in range(2):
            border[11 + n, x] = needed(int_rows, n, x).astype(F32)
        return 0

    lax.fori_loop(0, width_x // 4, lambda x, _: [rows(4 * x + i, 0) for i in range(4)][0], 0)
    for copy in started[first:]:
        copy.wait()


def pack(now, prev, vel, eps, delta, tilt, azimuth):
    width_x, width_y = vel.shape[0], vel.shape[1]
    planes = 4 * ITERS + 9 * (ITERS - 1)
    face = jax.ShapeDtypeStruct((planes, width_y, LANES), F32)
    return pl.pallas_call(
        pack_kernel,
        in_specs=any_specs(7),
        out_specs=[pl.BlockSpec(memory_space=pltpu.VMEM)] * 3,
        out_shape=(face, face, jax.ShapeDtypeStruct((13, width_x, REACH, LANES), F32)),
        scratch_shapes=[
            pltpu.VMEM((2, 2, ITERS - 1, width_y, LANES), jnp.int32),
            pltpu.VMEM((2, 4, width_x, TILE, LANES), F32),
            pltpu.VMEM((3, width_x, TILE, LANES), F32),
            pltpu.VMEM((2, width_x, TILE, LANES), jnp.int32),
            pltpu.SemaphoreType.DMA((33,)),
        ],
        compiler_params=pltpu.CompilerParams(vmem_limit_bytes=60 * MIB),
        cost_estimate=pl.CostEstimate(flops=1_000_000, bytes_accessed=8_000_000, transcendentals=0),
        name="pack_borders",
    )(now, prev, vel, eps, delta, tilt, azimuth)


def advance_inner(cover, now, prev, vel, eps, delta, tilt, azimuth, border):
    width_x, width_y = vel.shape[0], vel.shape[1]
    rows = width_y + REACH + 2
    half_x = width_x // 2
    shape = functools.partial(jax.ShapeDtypeStruct, dtype=F32)
    block = (half_x + 1, rows, SLOTS, LANES)
    part = shape((half_x - ITERS, width_y, LANES))
    vmem = lambda size: pltpu.VMEM(size, F32)
    return pl.pallas_call(
        inner_kernel,
        in_specs=[pl.BlockSpec(memory_space=pltpu.SMEM)] + any_specs(8),
        out_specs=any_specs(7),
        out_shape=(
            shape(now.shape),
            shape((ITERS,) + block[1:]),
            shape((ITERS + 1,) + block[1:]),
            shape((FACTORS, ITERS) + block[1:]),
            shape((2, ITERS, width_y, LANES)),
            part,
            part,
        ),
        scratch_shapes=[vmem(block)] * 4
        + [
            vmem((FACTORS, half_x) + block[1:]),
            vmem(vel.shape),
            vmem(now.shape[1:]),
            vmem(now.shape[1:]),
            vmem((3, width_x, width_y, LANES)),
            pltpu.VMEM((2, width_x, width_y, LANES), jnp.int32),
            vmem(border.shape),
            vmem((2, FACTORS + 1, rows, LANES)),
            pltpu.SemaphoreType.DMA((CHUNKS, 15)),
            pltpu.SemaphoreType.DMA((16,)),
            pltpu.SemaphoreType.DMA((width_x,)),
        ],
        compiler_params=pltpu.CompilerParams(vmem_limit_bytes=60 * MIB),
        cost_estimate=pl.CostEstimate(flops=80_000_000, bytes_accessed=200_000_000, transcendentals=0),
        name="inner_steps",
    )(cover, now, prev, vel, eps, delta, tilt, azimuth, border)


def advance_border(cover, edge_a, edge_b, edge_c, edge_corr, near, far, corner, wave):
    width_y = wave.shape[3]
    rows = width_y + REACH + 2
    block = (2 * ITERS + 1, rows, SLOTS, LANES)
    shape = functools.partial(jax.ShapeDtypeStruct, dtype=F32)
    vmem = lambda size: pltpu.VMEM(size, F32)
    return pl.pallas_call(
        border_kernel,
        in_specs=[pl.BlockSpec(memory_space=pltpu.SMEM)] + any_specs(8),
        out_specs=any_specs(3),
        out_shape=(shape(wave.shape), shape(edge_corr.shape), shape(edge_corr.shape)),
        scratch_shapes=[vmem(block)] * 4
        + [
            vmem((FACTORS,) + block),
            vmem(edge_corr.shape),
            vmem((2,) + near.shape),
            vmem(corner.shape),
            vmem((2, FACTORS + 1, rows, LANES)),
            vmem((2, 4, ITERS, width_y, LANES)),
            vmem(edge_corr.shape),
            pltpu.SemaphoreType.DMA((8,)),
        ],
        input_output_aliases={8: 0},
        compiler_params=pltpu.CompilerParams(vmem_limit_bytes=60 * MIB),
        cost_estimate=pl.CostEstimate(flops=20_000_000, bytes_accessed=20_000_000, transcendentals=0),
        name="border_steps",
    )(cover, edge_a, edge_b, edge_c, edge_corr, near, far, corner, wave)


def cut(array, start, size, axis):
    return lax.dynamic_slice_in_dim(array, start, size, axis=axis)


def other_rows(block, axis, second):
    return cut(block, (1 - second) * (block.shape[axis] - REACH), REACH, axis)


def swap_cores(rows):
    return lax.ppermute(rows, "gy", [(0, 1), (1, 0)])


def pairs_at(distance):
    return [(i, i ^ distance) for i in range(lax.axis_size("shot"))]


def scaled(block):
    return lax.optimization_barrier(block * (1.0 / ITERS))


def local(wave_now, wave_prev, vel_coef, epsilon, delta, tilt, azimuth, aperture):
    second = lax.axis_index("gy")
    columns = lax.axis_size("gx")
    inputs = (wave_now, wave_prev, vel_coef, epsilon, delta, tilt, azimuth)
    near, far, border = pack(*inputs)
    far = lax.ppermute(far, "gx", [(i, j) for i in range(1, columns - 1) for j in [i + 1 if i % 2 else i - 1]])
    near = lax.ppermute(near, "gx", [(i, i ^ 1) for i in range(columns) if i ^ 1 < columns])
    border = swap_cores(border)
    wave, edge_a, edge_b, edge_c, edge_corr, kept, sent = advance_inner(aperture, *inputs, border)
    received = lax.ppermute(sent, "shot", pairs_at(1))
    received, near, far = lax.optimization_barrier((received, near, far))
    held = scaled(kept) + received
    corner = swap_cores(jnp.stack([other_rows(f, 1, second) for f in (near, far)]))
    held, edge_corr = lax.optimization_barrier((held, edge_corr))
    wave, outside, outside_own = advance_border(aperture, edge_a, edge_b, edge_c, edge_corr, near, far, corner, wave)
    distance = 2
    while distance < lax.axis_size("shot"):
        held = held + lax.ppermute(held, "shot", pairs_at(distance))
        distance *= 2
    held, outside = lax.optimization_barrier((held, outside))
    distance = 1
    while distance < lax.axis_size("shot"):
        own = scaled(outside_own) if distance == 1 else outside
        outside = own + lax.ppermute(outside, "shot", pairs_at(distance))
        if distance == 1:
            held, outside = lax.optimization_barrier((held, outside))
            other = lax.ppermute(held, "shot", pairs_at(1))
        distance *= 2
    even = lax.axis_index("shot") % 2 == 0
    first, then = jnp.where(even, held, other), jnp.where(even, other, held)
    return wave, jnp.concatenate([outside[0], first, then, outside[1]])


def solution(mesh):
    return jax.shard_map(
        local,
        mesh=mesh,
        in_specs=(
            P("shot", None, "gx", "gy", None),
            P("shot", None, "gx", "gy", None),
            P("gx", "gy", None),
            P("gx", "gy", None),
            P("gx", "gy", None),
            P("gx", "gy", None),
            P("gx", "gy", None),
            P("shot", "gx", "gy"),
        ),
        out_specs=(P("shot", None, "gx", "gy", None), P("gx", "gy", None)),
        check_vma=False,
    )
```

```python
import functools
import math

import jax
import jax.numpy as jnp
from jax import lax
from jax.experimental import pallas as pl
from jax.experimental.pallas import tpu as pltpu
from jax.sharding import PartitionSpec as P

ITERS = 4
LANES = 128
TILE = 8
F32 = jnp.float32


def polynomial(square, start, terms):
    factors = [1.0]
    for k in range(start, start + 2 * terms, 2):
        factors.append(-factors[-1] / ((k + 1) * (k + 2)))
    result = factors[-1]
    for factor in factors[-2::-1]:
        result = factor + square * result
    return result


def sin_cos_near(degrees, terms):
    angle = degrees * (math.pi / 180.0)
    square = angle * angle
    return angle * polynomial(square, 1, terms), polynomial(square, 0, terms)


def sin_cos(degrees):
    quadrant = jnp.floor(degrees * (1.0 / 90.0) + 0.5)
    sine, cosine = sin_cos_near(degrees - 90.0 * quadrant, 4)
    odd = (quadrant == 1.0) | (quadrant == 3.0)
    first = jnp.where(odd, cosine, sine)
    second = jnp.where(odd, sine, cosine)
    back = (quadrant == 2.0) | (quadrant == 3.0)
    left = (quadrant == 1.0) | (quadrant == 2.0)
    return jnp.where(back, -first, first), jnp.where(left, -second, second)


def model_rows(vel, eps, delta, tilt, azimuth, mirrored):
    sin_t, cos_t = sin_cos_near(tilt, 5)
    sin_a, cos_a = sin_cos(azimuth)
    nx, ny, nz = sin_t * cos_a, sin_t * sin_a, cos_t
    gain = 1.0 + 2.0 * eps
    root = jnp.sqrt(1.0 + 2.0 * delta)
    half_x = (-0.5 if mirrored else 0.5) * nx
    return nx * nx, ny * ny, half_x * ny, half_x * nz, 0.5 * ny * nz, vel * gain, vel, vel * root


FACTORS = 7
SLOTS = 8
REACH = ITERS
CHUNKS = 4


def slot(half, field):
    return 4 * (field % 2) + 2 * half + field // 2


class Rows:
    def __init__(self, width_y, second):
        self.width_y = width_y
        self.total = width_y + REACH + 2
        self.own = 1 + REACH * second
        self.other = 1 + width_y * (1 - second)
        self.second = second

    def flat(self, plane, row, where, size):
        return pl.ds((plane * self.total + row) * SLOTS + where, size, stride=SLOTS)

    def tiles(self):
        return [slice(t, t + TILE) for t in range(0, self.width_y, TILE)]

    def pieces(self):
        return [(rows, TILE, self.own + rows.start) for rows in self.tiles()] + [(None, REACH, self.other)]


def z_terms(value, first_lane, last_lane):
    after = jnp.where(last_lane, 0.0, pltpu.roll(value, LANES - 1, 1))
    before = jnp.where(first_lane, 0.0, pltpu.roll(value, 1, 1))
    return after - before, after + before


def lane_ends(shape=(SLOTS, LANES)):
    lane = lax.broadcasted_iota(jnp.int32, shape, 1)
    return lane == 0, lane == LANES - 1


def sweep(old, new, slopes, sums, coef, planes, layout, step, done):
    count = layout.width_y + REACH - 1 - step
    first = 1 + (1 + step) * layout.second
    edges = lane_ends()
    is_q = lax.broadcasted_iota(jnp.int32, (SLOTS, LANES), 0) >= SLOTS // 2
    sign, weight = jnp.where(is_q, 1.0, -1.0), jnp.where(is_q, 2.0, 4.0)
    around = pl.ds(first - 1, count + 2)
    within = pl.ds(first, count)

    def plane(x):
        f_m, f_0, f_p = [old.at[x + i, around] for i in (-1, 0, 1)]
        g, h = slopes.at[pl.ds(x - 1, 3), around], sums.at[pl.ds(x, 2), around]
        out = new.at[x, within]
        factors = [coef.at[i, x, within] for i in range(FACTORS)]

        def column(j):
            below, above = f_m[j], f_p[j]
            g[2, j], h[1, j] = z_terms(above, *edges)
            return above - below, above + below, f_0[j], g[1, j]

        before, here = column(0), column(1)
        for j in range(count):
            after = column(j + 2)
            a, b, d, e, k, c1, c2 = [factor[j] for factor in factors]
            sum_z = h[0, j + 1]
            sum_y = after[2] + before[2]
            mixed = (
                (a * (here[1] - sum_z) + b * (sum_y - sum_z))
                + d * (after[0] - before[0])
                + (e * (g[2, j + 1] - g[0, j + 1]) + k * (after[3] - before[3]))
            )
            plain = jnp.where(is_q, sum_z, here[1] + sum_y) - weight * here[2]
            mine = plain + sign * mixed
            twice = here[2] + here[2]
            out[j] = (twice - out[j]) + (c1 * mine + c2 * pltpu.roll(mine, SLOTS // 2, 0))
            before, here = here, after
        done(x)

    for back in (1, 0):
        for j in range(count + 2):
            x, row = planes[0] - back, first - 1 + j
            slopes[x, row], sums[x, row] = z_terms(old[x, row], *edges)
    lax.fori_loop(*planes, lambda x, _: (plane(x), 0)[1], 0)


def seam(part, x, rows):
    low = lax.broadcasted_iota(jnp.int32, (SLOTS, LANES), 0) % 4 < 2
    for j in range(rows):
        value = part[x, j]
        part[x + 1, j] = jnp.where(low, pltpu.roll(value, SLOTS - 2, 0), pltpu.roll(value, 2, 0))


def clear_ends(refs, rows):
    for ref in refs:
        empty = jnp.zeros((ref.shape[0], 1) + ref.shape[2:], F32)
        ref[:, 0:1] = empty
        ref[:, rows - 1 : rows] = empty


def copies(pairs, sems, base=0):
    out = []
    for i, (source, target) in enumerate(pairs):
        out.append(pltpu.make_async_copy(source, target, sems.at[base + i]))
        out[-1].start()
    return out


def flat_view(ref):
    size = 1
    for length in ref.shape[:-1]:
        size *= length
    return ref.reshape(size, ref.shape[-1])


def put_model(natural, half, row, size, raw):
    for i, part in enumerate(model_rows(*raw, half == 1)):
        natural[half, i, row : row + size, :] = part


def spread_model(coef, natural, plane, layout):
    sublane = lax.broadcasted_iota(jnp.int32, (SLOTS, LANES), 0)
    is_q, is_mirrored = sublane >= SLOTS // 2, sublane % 4 >= 2

    def cell(i, row):
        low, high = [natural[half, i, pl.ds(row, SLOTS, stride=0), :] for half in range(2)]
        return jnp.where(is_mirrored, high, low)

    for begin, first, size in ((0, layout.own, layout.width_y), (layout.width_y, layout.other, REACH)):
        out = coef.at[:, plane, pl.ds(first, size)]
        for j in range(size):
            for i in range(5):
                out[i, j] = cell(i, begin + j)
            out[5, j] = jnp.where(is_q, cell(6, begin + j), cell(5, begin + j))
            out[6, j] = cell(7, begin + j)


def products(flat, layout, plane, half, rows):
    where = [layout.flat(plane, layout.own + rows.start, slot(half, field), TILE) for field in (0, 2)]
    return flat[where[0], :] * flat[where[1], :]


def inner_kernel(
    cover, now, prev, vel, eps, delta, tilt, azimuth, border,
    wave, edge_a, edge_b, edge_c, edge_corr, kept, sent,
    fa, fb, slopes, sums, coef, corr, in_now, in_prev, raw, raw_int, in_border, natural, load_sems, sems, wave_sems,
):
    second, odd = lax.axis_index("gy"), lax.axis_index("shot") % 2
    width_x, width_y = vel.shape[0], vel.shape[1]
    half_x = width_x // 2
    layout = Rows(width_y, second)
    rows = layout.total
    chunk = half_x // CHUNKS
    loads = []

    def load(c):
        pairs = [(border, in_border)] if c == 0 else []
        for start in (c * chunk, width_x - (c + 1) * chunk):
            at = pl.ds(start, chunk)
            pairs += [(now.at[0, :, at], in_now.at[:, at]), (prev.at[0, :, at], in_prev.at[:, at])]
            pairs += [(array.at[at], raw.at[n, at]) for n, array in enumerate((vel, eps, delta))]
            pairs += [(array.at[at], raw_int.at[n, at]) for n, array in enumerate((tilt, azimuth))]
        loads.append(copies(pairs, load_sems.at[c]))

    load(0)
    load(1)
    clear_ends((fa, fb), rows)

    def fill(i, _):
        for half in range(2):
            x = i if half == 0 else width_x - 1 - i
            for field in range(4):
                for own, size, row in layout.pieces():
                    spot = layout.flat(i, row, slot(half, field), size)
                    if own is None:
                        flat_view(fa)[spot, :] = in_border[field, x]
                        flat_view(fb)[spot, :] = in_border[4 + field, x]
                    else:
                        flat_view(fa)[spot, :] = in_now[field, x, own, :]
                        flat_view(fb)[spot, :] = in_prev[field, x, own, :]
        for half in range(2):
            x = i if half == 0 else width_x - 1 - i
            for own, size, row in layout.pieces():
                if own is None:
                    cells = [in_border[8 + n, x] for n in range(5)]
                else:
                    cells = [raw[n, x, own, :] for n in range(3)]
                    cells += [raw_int[n, x, own, :].astype(F32) for n in range(2)]
                put_model(natural, half, own.start if own else width_y, size, cells)
        spread_model(coef, natural, i, layout)
        return 0

    for c in range(CHUNKS):
        for copy in loads[c]:
            copy.wait()
        if c + 2 < CHUNKS:
            load(c + 2)
        lax.fori_loop(c * chunk, (c + 1) * chunk, fill, 0)
    out = copies([(coef.at[:, pl.ds(0, ITERS)], edge_c)], sems, 9)
    seam(fa, half_x - 1, rows)
    bufs = (fa, fb)
    covered = cover[0, 0, 0].astype(F32)
    scales = [jnp.where(odd == half, covered, covered / ITERS) for half in range(2)]

    def give_wave(i, half):
        x = i if half == 0 else width_x - 1 - i
        return pltpu.make_async_copy(in_now.at[:, x], wave.at[0, :, x], wave_sems.at[half * half_x + i])

    def finished(step):
        flat = flat_view(bufs[1 - step % 2])

        def done(i):
            for half in range(2):
                x = i if half == 0 else width_x - 1 - i
                for own in layout.tiles():
                    product = products(flat, layout, i, half, own)
                    total = product if step == 0 else corr[x, own, :] + product
                    corr[x, own, :] = scales[half] * total if step == ITERS - 1 else total
                    if step == ITERS - 1:
                        for field in range(4):
                            spot = layout.flat(i, layout.own + own.start, slot(half, field), TILE)
                            in_now[field, x, own, :] = flat[spot, :]
                if step == ITERS - 1:
                    give_wave(i, half).start()

        return done

    for step in range(ITERS):
        old, new = bufs[step % 2], bufs[1 - step % 2]
        sweep(old, new, slopes, sums, coef, (1 + step, half_x), layout, step, finished(step))
        if step < ITERS - 1:
            seam(new, half_x - 1, rows)
        if step == ITERS - 3:
            out += copies([(fa.at[pl.ds(0, ITERS)], edge_a)], sems, 10)
        if step == ITERS - 2:
            far = pl.ds(width_x - ITERS, ITERS)
            out += copies(
                [
                    (fb.at[pl.ds(0, ITERS + 1)], edge_b),
                    (corr.at[pl.ds(0, ITERS)], edge_corr.at[0]),
                    (corr.at[far], edge_corr.at[1]),
                ],
                sems,
                11,
            )
    part = half_x - ITERS
    out += copies(
        [
            (corr.at[pl.ds(ITERS + part * odd, part)], kept),
            (corr.at[pl.ds(ITERS + part * (1 - odd), part)], sent),
        ],
        sems,
        14,
    )
    for copy in out:
        copy.wait()
    for i in range(ITERS, half_x):
        for half in range(2):
            give_wave(i, half).wait()


def border_kernel(
    cover, edge_a, edge_b, edge_c, edge_corr, near, far, corner, wave_in,
    wave, image, image_own,
    fa, fb, slopes, sums, coef, corr, sides, corners, natural, in_now, picture, sems,
):
    second, odd = lax.axis_index("gy"), lax.axis_index("gx") % 2
    width_x, width_y = wave.shape[2], wave.shape[3]
    layout = Rows(width_y, second)
    rows = layout.total
    loads = copies(
        [
            (near, sides.at[1 - odd]),
            (far, sides.at[odd]),
            (corner.at[0], corners.at[1 - odd]),
            (corner.at[1], corners.at[odd]),
            (edge_a, fa.at[pl.ds(ITERS, ITERS)]),
            (edge_b, fb.at[pl.ds(ITERS, ITERS + 1)]),
            (edge_corr, corr),
            (edge_c, coef.at[:, pl.ds(ITERS, ITERS)]),
        ],
        sems,
    )
    clear_ends([ref.at[pl.ds(0, ITERS)] for ref in (fa, fb)], rows)
    for copy in loads[:4]:
        copy.wait()
    n_now, n_prev, less = 4 * ITERS, 4 * (ITERS - 1), ITERS - 1

    def cells(half, index, own):
        return corners[half, index] if own is None else sides[half, index, own, :]

    def fill(j, _):
        for half in range(2):
            nth = j if half == 0 else ITERS - 1 - j
            shorter = jnp.maximum(j - 1, 0) if half == 0 else jnp.minimum(ITERS - 1 - j, less - 1)
            for own, size, row in layout.pieces():
                for field in range(4):
                    spot = layout.flat(j, row, slot(half, field), size)
                    flat_view(fa)[spot, :] = cells(half, field * ITERS + nth, own)
                    flat_view(fb)[spot, :] = cells(half, n_now + field * less + shorter, own)
        for half in range(2):
            shorter = jnp.maximum(j - 1, 0) if half == 0 else jnp.minimum(ITERS - 1 - j, less - 1)
            for own, size, row in layout.pieces():
                raw = [cells(half, n_now + n_prev + n * less + shorter, own) for n in range(5)]
                put_model(natural, half, own.start if own else width_y, size, raw)
        spread_model(coef, natural, j, layout)
        return 0

    lax.fori_loop(0, ITERS, fill, 0)
    for copy in loads[4:]:
        copy.wait()

    corr[0, 0] = jnp.zeros(corr.shape[2:], F32)
    corr[1, ITERS - 1] = jnp.zeros(corr.shape[2:], F32)

    def finished(flat):
        def done(i):
            @pl.when(i >= ITERS)
            def _():
                for half in range(2):
                    x = i - ITERS if half == 0 else 2 * ITERS - 1 - i
                    for own in layout.tiles():
                        corr[half, x, own, :] = corr[half, x, own, :] + products(flat, layout, i, half, own)

        return done

    def advance(turn, _):
        for step, (old, new) in enumerate(((fa, fb), (fb, fa))):
            start = 1 + step + 2 * turn
            sweep(old, new, slopes, sums, coef, (start, start + ITERS), layout, 0, finished(flat_view(new)))
        return 0

    lax.fori_loop(0, ITERS // 2, advance, 0)
    corr[...] = cover[0, 0, 0].astype(F32) * corr[...]
    picture[...] = corr[...] * (1.0 / ITERS)
    out = copies([(picture, image), (corr, image_own)], sems)
    flat = flat_view(fa)

    def give(i, _):
        for half in range(2):
            x = i if half == 0 else ITERS - 1 - i
            for own in layout.tiles():
                for field in range(4):
                    spot = layout.flat(ITERS + i, layout.own + own.start, slot(half, field), TILE)
                    in_now[half, field, x, own, :] = flat[spot, :]
        return 0

    lax.fori_loop(0, ITERS, give, 0)
    out += copies(
        [
            (in_now.at[0], wave.at[0, :, pl.ds(0, ITERS)]),
            (in_now.at[1], wave.at[0, :, pl.ds(width_x - ITERS, ITERS)]),
        ],
        sems,
        2,
    )
    for copy in out:
        copy.wait()


def any_specs(count):
    return [pl.BlockSpec(memory_space=pl.ANY)] * count


MIB = 1024 * 1024


def pack_kernel(
    now, prev, vel, eps, delta, tilt, azimuth,
    near, far, border,
    planes_int, wave_rows, float_rows, int_rows, sems,
):
    second, odd = lax.axis_index("gy"), lax.axis_index("gx") % 2
    width_x, width_y = vel.shape[0], vel.shape[1]
    deep, less = ITERS, ITERS - 1
    n_now, n_prev = 4 * deep, 4 * less
    ints, floats = (tilt, azimuth), (vel, eps, delta)
    tile = pl.ds(pl.multiple_of((1 - second) * (width_y - TILE), TILE), TILE)
    pairs = [(array.at[0, :, :, tile], wave_rows.at[n]) for n, array in enumerate((now, prev))]
    pairs += [(array.at[:, tile], float_rows.at[n]) for n, array in enumerate(floats)]
    pairs += [(array.at[:, tile], int_rows.at[n]) for n, array in enumerate(ints)]
    ends = ((near, 1 - odd), (far, odd))
    for k, (_, high) in enumerate(ends):
        at = pl.ds(high * (width_x - less), less)
        pairs += [(ints[n].at[at], planes_int.at[k, n]) for n in range(2)]
    first = len(pairs)
    for out, high in ends:
        at = pl.ds(high * (width_x - less), less)
        for f in range(4):
            pairs.append((now.at[0, f, pl.ds(high * (width_x - deep), deep)], out.at[pl.ds(f * deep, deep)]))
            pairs.append((prev.at[0, f, at], out.at[pl.ds(n_now + f * less, less)]))
        for n in range(3):
            pairs.append((floats[n].at[at], out.at[pl.ds(n_now + n_prev + n * less, less)]))
    started = copies(pairs, sems)
    for copy in started[:first]:
        copy.wait()
    for k, (out, _) in enumerate(ends):
        for n in range(2):
            begin = n_now + n_prev + (3 + n) * less
            out[begin : begin + less] = planes_int[k, n].astype(F32)

    def needed(ref, *spot):
        return jnp.where(second == 1, ref[spot + (slice(0, REACH),)], ref[spot + (slice(TILE - REACH, TILE),)])

    def rows(x, _):
        for kind in range(2):
            for f in range(4):
                border[4 * kind + f, x] = needed(wave_rows, kind, f, x)
        for n in range(3):
            border[8 + n, x] = needed(float_rows, n, x)
        for n in range(2):
            border[11 + n, x] = needed(int_rows, n, x).astype(F32)
        return 0

    lax.fori_loop(0, width_x // 4, lambda x, _: [rows(4 * x + i, 0) for i in range(4)][0], 0)
    for copy in started[first:]:
        copy.wait()


def pack(now, prev, vel, eps, delta, tilt, azimuth):
    width_x, width_y = vel.shape[0], vel.shape[1]
    planes = 4 * ITERS + 9 * (ITERS - 1)
    face = jax.ShapeDtypeStruct((planes, width_y, LANES), F32)
    return pl.pallas_call(
        pack_kernel,
        in_specs=any_specs(7),
        out_specs=[pl.BlockSpec(memory_space=pltpu.VMEM)] * 3,
        out_shape=(face, face, jax.ShapeDtypeStruct((13, width_x, REACH, LANES), F32)),
        scratch_shapes=[
            pltpu.VMEM((2, 2, ITERS - 1, width_y, LANES), jnp.int32),
            pltpu.VMEM((2, 4, width_x, TILE, LANES), F32),
            pltpu.VMEM((3, width_x, TILE, LANES), F32),
            pltpu.VMEM((2, width_x, TILE, LANES), jnp.int32),
            pltpu.SemaphoreType.DMA((33,)),
        ],
        compiler_params=pltpu.CompilerParams(vmem_limit_bytes=60 * MIB),
        cost_estimate=pl.CostEstimate(flops=1_000_000, bytes_accessed=8_000_000, transcendentals=0),
        name="pack_borders",
    )(now, prev, vel, eps, delta, tilt, azimuth)


def advance_inner(cover, now, prev, vel, eps, delta, tilt, azimuth, border):
    width_x, width_y = vel.shape[0], vel.shape[1]
    rows = width_y + REACH + 2
    half_x = width_x // 2
    shape = functools.partial(jax.ShapeDtypeStruct, dtype=F32)
    block = (half_x + 1, rows, SLOTS, LANES)
    part = shape((half_x - ITERS, width_y, LANES))
    vmem = lambda size: pltpu.VMEM(size, F32)
    return pl.pallas_call(
        inner_kernel,
        in_specs=[pl.BlockSpec(memory_space=pltpu.SMEM)] + any_specs(8),
        out_specs=any_specs(7),
        out_shape=(
            shape(now.shape),
            shape((ITERS,) + block[1:]),
            shape((ITERS + 1,) + block[1:]),
            shape((FACTORS, ITERS) + block[1:]),
            shape((2, ITERS, width_y, LANES)),
            part,
            part,
        ),
        scratch_shapes=[vmem(block)] * 4
        + [
            vmem((FACTORS, half_x) + block[1:]),
            vmem(vel.shape),
            vmem(now.shape[1:]),
            vmem(now.shape[1:]),
            vmem((3, width_x, width_y, LANES)),
            pltpu.VMEM((2, width_x, width_y, LANES), jnp.int32),
            vmem(border.shape),
            vmem((2, FACTORS + 1, rows, LANES)),
            pltpu.SemaphoreType.DMA((CHUNKS, 15)),
            pltpu.SemaphoreType.DMA((16,)),
            pltpu.SemaphoreType.DMA((width_x,)),
        ],
        compiler_params=pltpu.CompilerParams(vmem_limit_bytes=60 * MIB),
        cost_estimate=pl.CostEstimate(flops=80_000_000, bytes_accessed=200_000_000, transcendentals=0),
        name="inner_steps",
    )(cover, now, prev, vel, eps, delta, tilt, azimuth, border)


def advance_border(cover, edge_a, edge_b, edge_c, edge_corr, near, far, corner, wave):
    width_y = wave.shape[3]
    rows = width_y + REACH + 2
    block = (2 * ITERS + 1, rows, SLOTS, LANES)
    shape = functools.partial(jax.ShapeDtypeStruct, dtype=F32)
    vmem = lambda size: pltpu.VMEM(size, F32)
    return pl.pallas_call(
        border_kernel,
        in_specs=[pl.BlockSpec(memory_space=pltpu.SMEM)] + any_specs(8),
        out_specs=any_specs(3),
        out_shape=(shape(wave.shape), shape(edge_corr.shape), shape(edge_corr.shape)),
        scratch_shapes=[vmem(block)] * 4
        + [
            vmem((FACTORS,) + block),
            vmem(edge_corr.shape),
            vmem((2,) + near.shape),
            vmem(corner.shape),
            vmem((2, FACTORS + 1, rows, LANES)),
            vmem((2, 4, ITERS, width_y, LANES)),
            vmem(edge_corr.shape),
            pltpu.SemaphoreType.DMA((8,)),
        ],
        input_output_aliases={8: 0},
        compiler_params=pltpu.CompilerParams(vmem_limit_bytes=60 * MIB),
        cost_estimate=pl.CostEstimate(flops=20_000_000, bytes_accessed=20_000_000, transcendentals=0),
        name="border_steps",
    )(cover, edge_a, edge_b, edge_c, edge_corr, near, far, corner, wave)


def cut(array, start, size, axis):
    return lax.dynamic_slice_in_dim(array, start, size, axis=axis)


def other_rows(block, axis, second):
    return cut(block, (1 - second) * (block.shape[axis] - REACH), REACH, axis)


def swap_cores(rows):
    return lax.ppermute(rows, "gy", [(0, 1), (1, 0)])


def pairs_at(distance):
    return [(i, i ^ distance) for i in range(lax.axis_size("shot"))]


def scaled(block):
    return lax.optimization_barrier(block * (1.0 / ITERS))


def local(wave_now, wave_prev, vel_coef, epsilon, delta, tilt, azimuth, aperture):
    second = lax.axis_index("gy")
    columns = lax.axis_size("gx")
    inputs = (wave_now, wave_prev, vel_coef, epsilon, delta, tilt, azimuth)
    near, far, border = pack(*inputs)
    near = lax.ppermute(near, "gx", [(i, i ^ 1) for i in range(columns) if i ^ 1 < columns])
    border = swap_cores(border)
    far, border = lax.optimization_barrier((far, border))
    far = lax.ppermute(far, "gx", [(i, j) for i in range(1, columns - 1) for j in [i + 1 if i % 2 else i - 1]])
    wave, edge_a, edge_b, edge_c, edge_corr, kept, sent = advance_inner(aperture, *inputs, border)
    received = lax.ppermute(sent, "shot", pairs_at(1))
    mine = scaled(kept)
    received, near, far = lax.optimization_barrier((received, near, far))
    corner = swap_cores(jnp.stack([other_rows(f, 1, second) for f in (near, far)]))
    received, corner = lax.optimization_barrier((received, corner))
    held = mine + received
    held, edge_corr = lax.optimization_barrier((held, edge_corr))
    wave, outside, outside_own = advance_border(aperture, edge_a, edge_b, edge_c, edge_corr, near, far, corner, wave)
    distance = 2
    while distance < lax.axis_size("shot"):
        held = held + lax.ppermute(held, "shot", pairs_at(distance))
        distance *= 2
    held, outside_own = lax.optimization_barrier((held, outside_own))
    own, distance = scaled(outside_own), 1
    while distance < lax.axis_size("shot"):
        own = outside = own + lax.ppermute(outside, "shot", pairs_at(distance))
        if distance == 1:
            held, own, outside = lax.optimization_barrier((held, own, outside))
            other = lax.ppermute(held, "shot", pairs_at(1))
        distance *= 2
    even = lax.axis_index("shot") % 2 == 0
    first, then = jnp.where(even, held, other), jnp.where(even, other, held)
    return wave, jnp.concatenate([outside[0], first, then, outside[1]])


def solution(mesh):
    return jax.shard_map(
        local,
        mesh=mesh,
        in_specs=(
            P("shot", None, "gx", "gy", None),
            P("shot", None, "gx", "gy", None),
            P("gx", "gy", None),
            P("gx", "gy", None),
            P("gx", "gy", None),
            P("gx", "gy", None),
            P("gx", "gy", None),
            P("shot", "gx", "gy"),
        ),
        out_specs=(P("shot", None, "gx", "gy", None), P("gx", "gy", None)),
        check_vma=False,
    )
```

```python
import functools
import math

import jax
import jax.numpy as jnp
from jax import lax
from jax.experimental import pallas as pl
from jax.experimental.pallas import tpu as pltpu
from jax.sharding import PartitionSpec as P

ITERS = 4
LANES = 128
TILE = 8
F32 = jnp.float32


def polynomial(square, start, terms):
    factors = [1.0]
    for k in range(start, start + 2 * terms, 2):
        factors.append(-factors[-1] / ((k + 1) * (k + 2)))
    result = factors[-1]
    for factor in factors[-2::-1]:
        result = factor + square * result
    return result


def sin_cos_near(degrees, terms):
    angle = degrees * (math.pi / 180.0)
    square = angle * angle
    return angle * polynomial(square, 1, terms), polynomial(square, 0, terms)


def sin_cos(degrees):
    quadrant = jnp.floor(degrees * (1.0 / 90.0) + 0.5)
    sine, cosine = sin_cos_near(degrees - 90.0 * quadrant, 4)
    odd = (quadrant == 1.0) | (quadrant == 3.0)
    first = jnp.where(odd, cosine, sine)
    second = jnp.where(odd, sine, cosine)
    back = (quadrant == 2.0) | (quadrant == 3.0)
    left = (quadrant == 1.0) | (quadrant == 2.0)
    return jnp.where(back, -first, first), jnp.where(left, -second, second)


def model_rows(vel, eps, delta, tilt, azimuth, mirrored):
    sin_t, cos_t = sin_cos_near(tilt, 5)
    sin_a, cos_a = sin_cos(azimuth)
    nx, ny, nz = sin_t * cos_a, sin_t * sin_a, cos_t
    gain = 1.0 + 2.0 * eps
    root = jnp.sqrt(1.0 + 2.0 * delta)
    half_x = (-0.5 if mirrored else 0.5) * nx
    return nx * nx, ny * ny, half_x * ny, half_x * nz, 0.5 * ny * nz, vel * gain, vel, vel * root


FACTORS = 7
SLOTS = 8
REACH = ITERS
CHUNKS = 4


def slot(half, field):
    return 4 * (field % 2) + 2 * half + field // 2


class Rows:
    def __init__(self, width_y, second):
        self.width_y = width_y
        self.total = width_y + REACH + 2
        self.own = 1 + REACH * second
        self.other = 1 + width_y * (1 - second)
        self.second = second

    def flat(self, plane, row, where, size):
        return pl.ds((plane * self.total + row) * SLOTS + where, size, stride=SLOTS)

    def tiles(self):
        return [slice(t, t + TILE) for t in range(0, self.width_y, TILE)]

    def pieces(self):
        return [(rows, TILE, self.own + rows.start) for rows in self.tiles()] + [(None, REACH, self.other)]


def z_terms(value, first_lane, last_lane):
    after = jnp.where(last_lane, 0.0, pltpu.roll(value, LANES - 1, 1))
    before = jnp.where(first_lane, 0.0, pltpu.roll(value, 1, 1))
    return after - before, after + before


def lane_ends(shape=(SLOTS, LANES)):
    lane = lax.broadcasted_iota(jnp.int32, shape, 1)
    return lane == 0, lane == LANES - 1


def sweep(old, new, slopes, sums, coef, planes, layout, step, done):
    count = layout.width_y + REACH - 1 - step
    first = 1 + (1 + step) * layout.second
    edges = lane_ends()
    is_q = lax.broadcasted_iota(jnp.int32, (SLOTS, LANES), 0) >= SLOTS // 2
    sign, weight = jnp.where(is_q, 1.0, -1.0), jnp.where(is_q, 2.0, 4.0)
    around = pl.ds(first - 1, count + 2)
    within = pl.ds(first, count)

    def plane(x):
        f_m, f_0, f_p = [old.at[x + i, around] for i in (-1, 0, 1)]
        g, h = slopes.at[pl.ds(x - 1, 3), around], sums.at[pl.ds(x, 2), around]
        out = new.at[x, within]
        factors = [coef.at[i, x, within] for i in range(FACTORS)]

        def column(j):
            below, above = f_m[j], f_p[j]
            g[2, j], h[1, j] = z_terms(above, *edges)
            return above - below, above + below, f_0[j], g[1, j]

        before, here = column(0), column(1)
        for j in range(count):
            after = column(j + 2)
            a, b, d, e, k, c1, c2 = [factor[j] for factor in factors]
            sum_z = h[0, j + 1]
            sum_y = after[2] + before[2]
            mixed = (
                (a * (here[1] - sum_z) + b * (sum_y - sum_z))
                + d * (after[0] - before[0])
                + (e * (g[2, j + 1] - g[0, j + 1]) + k * (after[3] - before[3]))
            )
            plain = jnp.where(is_q, sum_z, here[1] + sum_y) - weight * here[2]
            mine = plain + sign * mixed
            twice = here[2] + here[2]
            out[j] = (twice - out[j]) + (c1 * mine + c2 * pltpu.roll(mine, SLOTS // 2, 0))
            before, here = here, after
        done(x)

    for back in (1, 0):
        for j in range(count + 2):
            x, row = planes[0] - back, first - 1 + j
            slopes[x, row], sums[x, row] = z_terms(old[x, row], *edges)
    lax.fori_loop(*planes, lambda x, _: (plane(x), 0)[1], 0)


def seam(part, x, rows):
    low = lax.broadcasted_iota(jnp.int32, (SLOTS, LANES), 0) % 4 < 2
    for j in range(rows):
        value = part[x, j]
        part[x + 1, j] = jnp.where(low, pltpu.roll(value, SLOTS - 2, 0), pltpu.roll(value, 2, 0))


def clear_ends(refs, rows):
    for ref in refs:
        empty = jnp.zeros((ref.shape[0], 1) + ref.shape[2:], F32)
        ref[:, 0:1] = empty
        ref[:, rows - 1 : rows] = empty


def copies(pairs, sems, base=0):
    out = []
    for i, (source, target) in enumerate(pairs):
        out.append(pltpu.make_async_copy(source, target, sems.at[base + i]))
        out[-1].start()
    return out


def flat_view(ref):
    size = 1
    for length in ref.shape[:-1]:
        size *= length
    return ref.reshape(size, ref.shape[-1])


def put_model(natural, half, row, size, raw):
    for i, part in enumerate(model_rows(*raw, half == 1)):
        natural[half, i, row : row + size, :] = part


def spread_model(coef, natural, plane, layout):
    sublane = lax.broadcasted_iota(jnp.int32, (SLOTS, LANES), 0)
    is_q, is_mirrored = sublane >= SLOTS // 2, sublane % 4 >= 2

    def cell(i, row):
        low, high = [natural[half, i, pl.ds(row, SLOTS, stride=0), :] for half in range(2)]
        return jnp.where(is_mirrored, high, low)

    for begin, first, size in ((0, layout.own, layout.width_y), (layout.width_y, layout.other, REACH)):
        out = coef.at[:, plane, pl.ds(first, size)]
        for j in range(size):
            for i in range(5):
                out[i, j] = cell(i, begin + j)
            out[5, j] = jnp.where(is_q, cell(6, begin + j), cell(5, begin + j))
            out[6, j] = cell(7, begin + j)


def products(flat, layout, plane, half, rows):
    where = [layout.flat(plane, layout.own + rows.start, slot(half, field), TILE) for field in (0, 2)]
    return flat[where[0], :] * flat[where[1], :]


def inner_kernel(
    cover, now, prev, vel, eps, delta, tilt, azimuth, border,
    wave, edge_a, edge_b, edge_c, edge_corr, kept, sent,
    fa, fb, slopes, sums, coef, corr, in_now, in_prev, raw, raw_int, in_border, natural, load_sems, sems, wave_sems,
):
    second, odd = lax.axis_index("gy"), lax.axis_index("shot") % 2
    width_x, width_y = vel.shape[0], vel.shape[1]
    half_x = width_x // 2
    layout = Rows(width_y, second)
    rows = layout.total
    chunk = half_x // CHUNKS
    loads = []

    def load(c):
        pairs = [(border, in_border)] if c == 0 else []
        for start in (c * chunk, width_x - (c + 1) * chunk):
            at = pl.ds(start, chunk)
            pairs += [(now.at[0, :, at], in_now.at[:, at]), (prev.at[0, :, at], in_prev.at[:, at])]
            pairs += [(array.at[at], raw.at[n, at]) for n, array in enumerate((vel, eps, delta))]
            pairs += [(array.at[at], raw_int.at[n, at]) for n, array in enumerate((tilt, azimuth))]
        loads.append(copies(pairs, load_sems.at[c]))

    load(0)
    load(1)
    clear_ends((fa, fb), rows)

    def fill(i, _):
        for half in range(2):
            x = i if half == 0 else width_x - 1 - i
            for field in range(4):
                for own, size, row in layout.pieces():
                    spot = layout.flat(i, row, slot(half, field), size)
                    if own is None:
                        flat_view(fa)[spot, :] = in_border[field, x]
                        flat_view(fb)[spot, :] = in_border[4 + field, x]
                    else:
                        flat_view(fa)[spot, :] = in_now[field, x, own, :]
                        flat_view(fb)[spot, :] = in_prev[field, x, own, :]
        for half in range(2):
            x = i if half == 0 else width_x - 1 - i
            for own, size, row in layout.pieces():
                if own is None:
                    cells = [in_border[8 + n, x] for n in range(5)]
                else:
                    cells = [raw[n, x, own, :] for n in range(3)]
                    cells += [raw_int[n, x, own, :].astype(F32) for n in range(2)]
                put_model(natural, half, own.start if own else width_y, size, cells)
        spread_model(coef, natural, i, layout)
        return 0

    for c in range(CHUNKS):
        for copy in loads[c]:
            copy.wait()
        if c + 2 < CHUNKS:
            load(c + 2)
        lax.fori_loop(c * chunk, (c + 1) * chunk, fill, 0)
    out = copies([(coef.at[:, pl.ds(0, ITERS)], edge_c)], sems, 9)
    seam(fa, half_x - 1, rows)
    bufs = (fa, fb)
    covered = cover[0, 0, 0].astype(F32)
    scales = [jnp.where(odd == half, covered, covered / ITERS) for half in range(2)]

    def give_wave(i, half):
        x = i if half == 0 else width_x - 1 - i
        return pltpu.make_async_copy(in_now.at[:, x], wave.at[0, :, x], wave_sems.at[half * half_x + i])

    def finished(step):
        flat = flat_view(bufs[1 - step % 2])

        def done(i):
            for half in range(2):
                x = i if half == 0 else width_x - 1 - i
                for own in layout.tiles():
                    product = products(flat, layout, i, half, own)
                    total = product if step == 0 else corr[x, own, :] + product
                    corr[x, own, :] = scales[half] * total if step == ITERS - 1 else total
                    if step == ITERS - 1:
                        for field in range(4):
                            spot = layout.flat(i, layout.own + own.start, slot(half, field), TILE)
                            in_now[field, x, own, :] = flat[spot, :]
                if step == ITERS - 1:
                    give_wave(i, half).start()

        return done

    for step in range(ITERS):
        old, new = bufs[step % 2], bufs[1 - step % 2]
        sweep(old, new, slopes, sums, coef, (1 + step, half_x), layout, step, finished(step))
        if step < ITERS - 1:
            seam(new, half_x - 1, rows)
        if step == ITERS - 3:
            out += copies([(fa.at[pl.ds(0, ITERS)], edge_a)], sems, 10)
        if step == ITERS - 2:
            far = pl.ds(width_x - ITERS, ITERS)
            out += copies(
                [
                    (fb.at[pl.ds(0, ITERS + 1)], edge_b),
                    (corr.at[pl.ds(0, ITERS)], edge_corr.at[0]),
                    (corr.at[far], edge_corr.at[1]),
                ],
                sems,
                11,
            )
    part = half_x - ITERS
    out += copies(
        [
            (corr.at[pl.ds(ITERS + part * odd, part)], kept),
            (corr.at[pl.ds(ITERS + part * (1 - odd), part)], sent),
        ],
        sems,
        14,
    )
    for copy in out:
        copy.wait()
    for i in range(ITERS, half_x):
        for half in range(2):
            give_wave(i, half).wait()


def border_kernel(
    cover, edge_a, edge_b, edge_c, edge_corr, near, far, corner, wave_in,
    wave, image, image_own,
    fa, fb, slopes, sums, coef, corr, sides, corners, natural, in_now, picture, sems,
):
    second, odd = lax.axis_index("gy"), lax.axis_index("gx") % 2
    width_x, width_y = wave.shape[2], wave.shape[3]
    layout = Rows(width_y, second)
    rows = layout.total
    parts = []
    for begin, end in ((0, ITERS // 2), (ITERS // 2, ITERS)):
        more = (begin + 1 if begin else 0, end + 1)
        parts.append(
            [
                (edge_a.at[pl.ds(begin, end - begin)], fa.at[pl.ds(ITERS + begin, end - begin)]),
                (edge_b.at[pl.ds(more[0], more[1] - more[0])], fb.at[pl.ds(ITERS + more[0], more[1] - more[0])]),
                (edge_c.at[:, pl.ds(begin, end - begin)], coef.at[:, pl.ds(ITERS + begin, end - begin)]),
            ]
        )
    loads = copies(
        [
            (near, sides.at[1 - odd]),
            (far, sides.at[odd]),
            (corner.at[0], corners.at[1 - odd]),
            (corner.at[1], corners.at[odd]),
            (edge_corr, corr),
        ]
        + parts[0]
        + parts[1],
        sems,
    )
    clear_ends([ref.at[pl.ds(0, ITERS)] for ref in (fa, fb)], rows)
    for copy in loads[:4]:
        copy.wait()
    n_now, n_prev, less = 4 * ITERS, 4 * (ITERS - 1), ITERS - 1

    def cells(half, index, own):
        return corners[half, index] if own is None else sides[half, index, own, :]

    def fill(j, _):
        for half in range(2):
            nth = j if half == 0 else ITERS - 1 - j
            shorter = jnp.maximum(j - 1, 0) if half == 0 else jnp.minimum(ITERS - 1 - j, less - 1)
            for own, size, row in layout.pieces():
                for field in range(4):
                    spot = layout.flat(j, row, slot(half, field), size)
                    flat_view(fa)[spot, :] = cells(half, field * ITERS + nth, own)
                    flat_view(fb)[spot, :] = cells(half, n_now + field * less + shorter, own)
        for half in range(2):
            shorter = jnp.maximum(j - 1, 0) if half == 0 else jnp.minimum(ITERS - 1 - j, less - 1)
            for own, size, row in layout.pieces():
                raw = [cells(half, n_now + n_prev + n * less + shorter, own) for n in range(5)]
                put_model(natural, half, own.start if own else width_y, size, raw)
        spread_model(coef, natural, j, layout)
        return 0

    lax.fori_loop(0, ITERS, fill, 0)
    for copy in loads[4:8]:
        copy.wait()

    corr[0, 0] = jnp.zeros(corr.shape[2:], F32)
    corr[1, ITERS - 1] = jnp.zeros(corr.shape[2:], F32)

    def finished(flat):
        def done(i):
            @pl.when(i >= ITERS)
            def _():
                for half in range(2):
                    x = i - ITERS if half == 0 else 2 * ITERS - 1 - i
                    for own in layout.tiles():
                        corr[half, x, own, :] = corr[half, x, own, :] + products(flat, layout, i, half, own)

        return done

    def advance(turn, _):
        @pl.when(turn == 1)
        def _():
            for copy in loads[8:]:
                copy.wait()

        for step, (old, new) in enumerate(((fa, fb), (fb, fa))):
            start = 1 + step + 2 * turn
            sweep(old, new, slopes, sums, coef, (start, start + ITERS), layout, 0, finished(flat_view(new)))
        return 0

    lax.fori_loop(0, ITERS // 2, advance, 0)
    corr[...] = cover[0, 0, 0].astype(F32) * corr[...]
    picture[...] = corr[...] * (1.0 / ITERS)
    out = copies([(picture, image), (corr, image_own)], sems)
    flat = flat_view(fa)

    def give(i, _):
        for half in range(2):
            x = i if half == 0 else ITERS - 1 - i
            for own in layout.tiles():
                for field in range(4):
                    spot = layout.flat(ITERS + i, layout.own + own.start, slot(half, field), TILE)
                    in_now[half, field, x, own, :] = flat[spot, :]
        return 0

    lax.fori_loop(0, ITERS, give, 0)
    out += copies(
        [
            (in_now.at[0], wave.at[0, :, pl.ds(0, ITERS)]),
            (in_now.at[1], wave.at[0, :, pl.ds(width_x - ITERS, ITERS)]),
        ],
        sems,
        2,
    )
    for copy in out:
        copy.wait()


def any_specs(count):
    return [pl.BlockSpec(memory_space=pl.ANY)] * count


MIB = 1024 * 1024


def pack_kernel(
    now, prev, vel, eps, delta, tilt, azimuth,
    near, far, border,
    planes_int, wave_rows, float_rows, int_rows, sems,
):
    second, odd = lax.axis_index("gy"), lax.axis_index("gx") % 2
    width_x, width_y = vel.shape[0], vel.shape[1]
    deep, less = ITERS, ITERS - 1
    n_now, n_prev = 4 * deep, 4 * less
    ints, floats = (tilt, azimuth), (vel, eps, delta)
    tile = pl.ds(pl.multiple_of((1 - second) * (width_y - TILE), TILE), TILE)
    pairs = [(array.at[0, :, :, tile], wave_rows.at[n]) for n, array in enumerate((now, prev))]
    pairs += [(array.at[:, tile], float_rows.at[n]) for n, array in enumerate(floats)]
    pairs += [(array.at[:, tile], int_rows.at[n]) for n, array in enumerate(ints)]
    ends = ((near, 1 - odd), (far, odd))
    for k, (_, high) in enumerate(ends):
        at = pl.ds(high * (width_x - less), less)
        pairs += [(ints[n].at[at], planes_int.at[k, n]) for n in range(2)]
    first = len(pairs)
    for out, high in ends:
        at = pl.ds(high * (width_x - less), less)
        for f in range(4):
            pairs.append((now.at[0, f, pl.ds(high * (width_x - deep), deep)], out.at[pl.ds(f * deep, deep)]))
            pairs.append((prev.at[0, f, at], out.at[pl.ds(n_now + f * less, less)]))
        for n in range(3):
            pairs.append((floats[n].at[at], out.at[pl.ds(n_now + n_prev + n * less, less)]))
    started = copies(pairs, sems)
    for copy in started[:first]:
        copy.wait()
    for k, (out, _) in enumerate(ends):
        for n in range(2):
            begin = n_now + n_prev + (3 + n) * less
            out[begin : begin + less] = planes_int[k, n].astype(F32)

    def needed(ref, *spot):
        return ref[spot + (pl.ds(REACH * (1 - second), REACH), slice(None))]

    def rows(x, _):
        for kind in range(2):
            for f in range(4):
                border[4 * kind + f, x] = needed(wave_rows, kind, f, x)
        for n in range(3):
            border[8 + n, x] = needed(float_rows, n, x)
        for n in range(2):
            border[11 + n, x] = needed(int_rows, n, x).astype(F32)
        return 0

    lax.fori_loop(0, width_x // 4, lambda x, _: [rows(4 * x + i, 0) for i in range(4)][0], 0)
    for copy in started[first:]:
        copy.wait()


def pack(now, prev, vel, eps, delta, tilt, azimuth):
    width_x, width_y = vel.shape[0], vel.shape[1]
    planes = 4 * ITERS + 9 * (ITERS - 1)
    face = jax.ShapeDtypeStruct((planes, width_y, LANES), F32)
    return pl.pallas_call(
        pack_kernel,
        in_specs=any_specs(7),
        out_specs=[pl.BlockSpec(memory_space=pltpu.VMEM)] * 3,
        out_shape=(face, face, jax.ShapeDtypeStruct((13, width_x, REACH, LANES), F32)),
        scratch_shapes=[
            pltpu.VMEM((2, 2, ITERS - 1, width_y, LANES), jnp.int32),
            pltpu.VMEM((2, 4, width_x, TILE, LANES), F32),
            pltpu.VMEM((3, width_x, TILE, LANES), F32),
            pltpu.VMEM((2, width_x, TILE, LANES), jnp.int32),
            pltpu.SemaphoreType.DMA((33,)),
        ],
        compiler_params=pltpu.CompilerParams(vmem_limit_bytes=60 * MIB),
        cost_estimate=pl.CostEstimate(flops=1_000_000, bytes_accessed=8_000_000, transcendentals=0),
        name="pack_borders",
    )(now, prev, vel, eps, delta, tilt, azimuth)


def advance_inner(cover, now, prev, vel, eps, delta, tilt, azimuth, border):
    width_x, width_y = vel.shape[0], vel.shape[1]
    rows = width_y + REACH + 2
    half_x = width_x // 2
    shape = functools.partial(jax.ShapeDtypeStruct, dtype=F32)
    block = (half_x + 1, rows, SLOTS, LANES)
    part = shape((half_x - ITERS, width_y, LANES))
    vmem = lambda size: pltpu.VMEM(size, F32)
    return pl.pallas_call(
        inner_kernel,
        in_specs=[pl.BlockSpec(memory_space=pltpu.SMEM)] + any_specs(8),
        out_specs=any_specs(7),
        out_shape=(
            shape(now.shape),
            shape((ITERS,) + block[1:]),
            shape((ITERS + 1,) + block[1:]),
            shape((FACTORS, ITERS) + block[1:]),
            shape((2, ITERS, width_y, LANES)),
            part,
            part,
        ),
        scratch_shapes=[vmem(block)] * 4
        + [
            vmem((FACTORS, half_x) + block[1:]),
            vmem(vel.shape),
            vmem(now.shape[1:]),
            vmem(now.shape[1:]),
            vmem((3, width_x, width_y, LANES)),
            pltpu.VMEM((2, width_x, width_y, LANES), jnp.int32),
            vmem(border.shape),
            vmem((2, FACTORS + 1, rows + TILE, LANES)),
            pltpu.SemaphoreType.DMA((CHUNKS, 15)),
            pltpu.SemaphoreType.DMA((16,)),
            pltpu.SemaphoreType.DMA((width_x,)),
        ],
        compiler_params=pltpu.CompilerParams(vmem_limit_bytes=60 * MIB),
        cost_estimate=pl.CostEstimate(flops=80_000_000, bytes_accessed=200_000_000, transcendentals=0),
        name="inner_steps",
    )(cover, now, prev, vel, eps, delta, tilt, azimuth, border)


def advance_border(cover, edge_a, edge_b, edge_c, edge_corr, near, far, corner, wave):
    width_y = wave.shape[3]
    rows = width_y + REACH + 2
    block = (2 * ITERS + 1, rows, SLOTS, LANES)
    shape = functools.partial(jax.ShapeDtypeStruct, dtype=F32)
    vmem = lambda size: pltpu.VMEM(size, F32)
    return pl.pallas_call(
        border_kernel,
        in_specs=[pl.BlockSpec(memory_space=pltpu.SMEM)] + any_specs(8),
        out_specs=any_specs(3),
        out_shape=(shape(wave.shape), shape(edge_corr.shape), shape(edge_corr.shape)),
        scratch_shapes=[vmem(block)] * 4
        + [
            vmem((FACTORS,) + block),
            vmem(edge_corr.shape),
            vmem((2,) + near.shape),
            vmem(corner.shape),
            vmem((2, FACTORS + 1, rows + TILE, LANES)),
            vmem((2, 4, ITERS, width_y, LANES)),
            vmem(edge_corr.shape),
            pltpu.SemaphoreType.DMA((11,)),
        ],
        input_output_aliases={8: 0},
        compiler_params=pltpu.CompilerParams(vmem_limit_bytes=60 * MIB),
        cost_estimate=pl.CostEstimate(flops=20_000_000, bytes_accessed=20_000_000, transcendentals=0),
        name="border_steps",
    )(cover, edge_a, edge_b, edge_c, edge_corr, near, far, corner, wave)


def cut(array, start, size, axis):
    return lax.dynamic_slice_in_dim(array, start, size, axis=axis)


def other_rows(block, axis, second):
    return cut(block, (1 - second) * (block.shape[axis] - REACH), REACH, axis)


def swap_cores(rows):
    return lax.ppermute(rows, "gy", [(0, 1), (1, 0)])


def pairs_at(distance):
    return [(i, i ^ distance) for i in range(lax.axis_size("shot"))]


def scaled(block):
    return lax.optimization_barrier(block * (1.0 / ITERS))


def local(wave_now, wave_prev, vel_coef, epsilon, delta, tilt, azimuth, aperture):
    second = lax.axis_index("gy")
    columns = lax.axis_size("gx")
    inputs = (wave_now, wave_prev, vel_coef, epsilon, delta, tilt, azimuth)
    near, far, border = pack(*inputs)
    near = lax.ppermute(near, "gx", [(i, i ^ 1) for i in range(columns) if i ^ 1 < columns])
    border = swap_cores(border)
    far, border = lax.optimization_barrier((far, border))
    far = lax.ppermute(far, "gx", [(i, j) for i in range(1, columns - 1) for j in [i + 1 if i % 2 else i - 1]])
    wave, edge_a, edge_b, edge_c, edge_corr, kept, sent = advance_inner(aperture, *inputs, border)
    received = lax.ppermute(sent, "shot", pairs_at(1))
    mine = scaled(kept)
    received, near, far = lax.optimization_barrier((received, near, far))
    corner = swap_cores(jnp.stack([other_rows(f, 1, second) for f in (near, far)]))
    received, corner = lax.optimization_barrier((received, corner))
    held = mine + received
    held, edge_corr = lax.optimization_barrier((held, edge_corr))
    wave, outside, outside_own = advance_border(aperture, edge_a, edge_b, edge_c, edge_corr, near, far, corner, wave)
    distance = 2
    while distance < lax.axis_size("shot"):
        held = held + lax.ppermute(held, "shot", pairs_at(distance))
        distance *= 2
    held, outside_own = lax.optimization_barrier((held, outside_own))
    own, distance = scaled(outside_own), 1
    while distance < lax.axis_size("shot"):
        own = outside = own + lax.ppermute(outside, "shot", pairs_at(distance))
        if distance == 1:
            held, own, outside = lax.optimization_barrier((held, own, outside))
            other = lax.ppermute(held, "shot", pairs_at(1))
        distance *= 2
    even = lax.axis_index("shot") % 2 == 0
    first, then = jnp.where(even, held, other), jnp.where(even, other, held)
    return wave, jnp.concatenate([outside[0], first, then, outside[1]])


def solution(mesh):
    return jax.shard_map(
        local,
        mesh=mesh,
        in_specs=(
            P("shot", None, "gx", "gy", None),
            P("shot", None, "gx", "gy", None),
            P("gx", "gy", None),
            P("gx", "gy", None),
            P("gx", "gy", None),
            P("gx", "gy", None),
            P("gx", "gy", None),
            P("shot", "gx", "gy"),
        ),
        out_specs=(P("shot", None, "gx", "gy", None), P("gx", "gy", None)),
        check_vma=False,
    )
```

```python
import functools
import math

import jax
import jax.numpy as jnp
from jax import lax
from jax.experimental import pallas as pl
from jax.experimental.pallas import tpu as pltpu
from jax.sharding import PartitionSpec as P

ITERS = 4
LANES = 128
TILE = 8
F32 = jnp.float32


def polynomial(square, start, terms):
    factors = [1.0]
    for k in range(start, start + 2 * terms, 2):
        factors.append(-factors[-1] / ((k + 1) * (k + 2)))
    result = factors[-1]
    for factor in factors[-2::-1]:
        result = factor + square * result
    return result


def sin_cos_near(degrees, terms):
    angle = degrees * (math.pi / 180.0)
    square = angle * angle
    return angle * polynomial(square, 1, terms), polynomial(square, 0, terms)


def sin_cos(degrees):
    quadrant = jnp.floor(degrees * (1.0 / 90.0) + 0.5)
    sine, cosine = sin_cos_near(degrees - 90.0 * quadrant, 4)
    odd = (quadrant == 1.0) | (quadrant == 3.0)
    first = jnp.where(odd, cosine, sine)
    second = jnp.where(odd, sine, cosine)
    back = (quadrant == 2.0) | (quadrant == 3.0)
    left = (quadrant == 1.0) | (quadrant == 2.0)
    return jnp.where(back, -first, first), jnp.where(left, -second, second)


def model_rows(vel, eps, delta, tilt, azimuth, mirrored):
    sin_t, cos_t = sin_cos_near(tilt, 5)
    sin_a, cos_a = sin_cos(azimuth)
    nx, ny, nz = sin_t * cos_a, sin_t * sin_a, cos_t
    gain = 1.0 + 2.0 * eps
    root = jnp.sqrt(1.0 + 2.0 * delta)
    half_x = (-0.5 if mirrored else 0.5) * nx
    return nx * nx, ny * ny, half_x * ny, half_x * nz, 0.5 * ny * nz, vel * gain, vel, vel * root


FACTORS = 7
SLOTS = 8
REACH = ITERS
CHUNKS = 4


def slot(half, field):
    return 4 * (field % 2) + 2 * half + field // 2


class Rows:
    def __init__(self, width_y, second):
        self.width_y = width_y
        self.total = width_y + REACH + 2
        self.own = 1 + REACH * second
        self.other = 1 + width_y * (1 - second)
        self.second = second

    def flat(self, plane, row, where, size):
        return pl.ds((plane * self.total + row) * SLOTS + where, size, stride=SLOTS)

    def tiles(self):
        return [slice(t, t + TILE) for t in range(0, self.width_y, TILE)]

    def pieces(self):
        return [(rows, TILE, self.own + rows.start) for rows in self.tiles()] + [(None, REACH, self.other)]


def z_terms(value, first_lane, last_lane):
    after = jnp.where(last_lane, 0.0, pltpu.roll(value, LANES - 1, 1))
    before = jnp.where(first_lane, 0.0, pltpu.roll(value, 1, 1))
    return after - before, after + before


def lane_ends(shape=(SLOTS, LANES)):
    lane = lax.broadcasted_iota(jnp.int32, shape, 1)
    return lane == 0, lane == LANES - 1


def sweep(old, new, slopes, sums, coef, planes, layout, step, done):
    count = layout.width_y + REACH - 1 - step
    first = 1 + (1 + step) * layout.second
    edges = lane_ends()
    is_q = lax.broadcasted_iota(jnp.int32, (SLOTS, LANES), 0) >= SLOTS // 2
    sign, weight = jnp.where(is_q, 1.0, -1.0), jnp.where(is_q, 2.0, 4.0)
    around = pl.ds(first - 1, count + 2)
    within = pl.ds(first, count)

    def plane(x):
        f_m, f_0, f_p = [old.at[x + i, around] for i in (-1, 0, 1)]
        g, h = slopes.at[pl.ds(x - 1, 3), around], sums.at[pl.ds(x, 2), around]
        out = new.at[x, within]
        factors = [coef.at[i, x, within] for i in range(FACTORS)]

        def column(j):
            below, above = f_m[j], f_p[j]
            g[2, j], h[1, j] = z_terms(above, *edges)
            return above - below, above + below, f_0[j], g[1, j]

        before, here = column(0), column(1)
        for j in range(count):
            after = column(j + 2)
            a, b, d, e, k, c1, c2 = [factor[j] for factor in factors]
            sum_z = h[0, j + 1]
            sum_y = after[2] + before[2]
            mixed = (
                (a * (here[1] - sum_z) + b * (sum_y - sum_z))
                + d * (after[0] - before[0])
                + (e * (g[2, j + 1] - g[0, j + 1]) + k * (after[3] - before[3]))
            )
            plain = jnp.where(is_q, sum_z, here[1] + sum_y) - weight * here[2]
            mine = plain + sign * mixed
            twice = here[2] + here[2]
            out[j] = (twice - out[j]) + (c1 * mine + c2 * pltpu.roll(mine, SLOTS // 2, 0))
            before, here = here, after
        done(x)

    for back in (1, 0):
        for j in range(count + 2):
            x, row = planes[0] - back, first - 1 + j
            slopes[x, row], sums[x, row] = z_terms(old[x, row], *edges)
    lax.fori_loop(*planes, lambda x, _: (plane(x), 0)[1], 0)


def seam(part, x, rows):
    low = lax.broadcasted_iota(jnp.int32, (SLOTS, LANES), 0) % 4 < 2
    for j in range(rows):
        value = part[x, j]
        part[x + 1, j] = jnp.where(low, pltpu.roll(value, SLOTS - 2, 0), pltpu.roll(value, 2, 0))


def clear_ends(refs, rows):
    for ref in refs:
        empty = jnp.zeros((ref.shape[0], 1) + ref.shape[2:], F32)
        ref[:, 0:1] = empty
        ref[:, rows - 1 : rows] = empty


def copies(pairs, sems, base=0):
    out = []
    for i, (source, target) in enumerate(pairs):
        out.append(pltpu.make_async_copy(source, target, sems.at[base + i]))
        out[-1].start()
    return out


def flat_view(ref):
    size = 1
    for length in ref.shape[:-1]:
        size *= length
    return ref.reshape(size, ref.shape[-1])


def put_model(natural, half, row, size, raw):
    for i, part in enumerate(model_rows(*raw, half == 1)):
        natural[half, i, row : row + size, :] = part


def spread_model(coef, natural, plane, layout):
    sublane = lax.broadcasted_iota(jnp.int32, (SLOTS, LANES), 0)
    is_q, is_mirrored = sublane >= SLOTS // 2, sublane % 4 >= 2

    def cell(i, row):
        low, high = [natural[half, i, pl.ds(row, SLOTS, stride=0), :] for half in range(2)]
        return jnp.where(is_mirrored, high, low)

    for begin, first, size in ((0, layout.own, layout.width_y), (layout.width_y, layout.other, REACH)):
        out = coef.at[:, plane, pl.ds(first, size)]
        for j in range(size):
            for i in range(5):
                out[i, j] = cell(i, begin + j)
            out[5, j] = jnp.where(is_q, cell(6, begin + j), cell(5, begin + j))
            out[6, j] = cell(7, begin + j)


def products(flat, layout, plane, half, rows):
    where = [layout.flat(plane, layout.own + rows.start, slot(half, field), TILE) for field in (0, 2)]
    return flat[where[0], :] * flat[where[1], :]


def inner_kernel(
    cover, now, prev, vel, eps, delta, tilt, azimuth, border,
    wave, edge_a, edge_b, edge_c, edge_corr, kept, sent,
    fa, fb, slopes, sums, coef, corr, in_now, in_prev, raw, raw_int, in_border, natural, load_sems, sems, wave_sems,
):
    second, odd = lax.axis_index("gy"), lax.axis_index("shot") % 2
    width_x, width_y = vel.shape[0], vel.shape[1]
    half_x = width_x // 2
    layout = Rows(width_y, second)
    rows = layout.total
    chunk = half_x // CHUNKS
    loads = []

    def load(c):
        pairs = [(border, in_border)] if c == 0 else []
        for start in (c * chunk, width_x - (c + 1) * chunk):
            at = pl.ds(start, chunk)
            pairs += [(now.at[0, :, at], in_now.at[:, at]), (prev.at[0, :, at], in_prev.at[:, at])]
            pairs += [(array.at[at], raw.at[n, at]) for n, array in enumerate((vel, eps, delta))]
            pairs += [(array.at[at], raw_int.at[n, at]) for n, array in enumerate((tilt, azimuth))]
        loads.append(copies(pairs, load_sems.at[c]))

    load(0)
    load(1)
    clear_ends((fa, fb), rows)

    def fill(i, _):
        for half in range(2):
            x = i if half == 0 else width_x - 1 - i
            for field in range(4):
                for own, size, row in layout.pieces():
                    spot = layout.flat(i, row, slot(half, field), size)
                    if own is None:
                        flat_view(fa)[spot, :] = in_border[field, x]
                        flat_view(fb)[spot, :] = in_border[4 + field, x]
                    else:
                        flat_view(fa)[spot, :] = in_now[field, x, own, :]
                        flat_view(fb)[spot, :] = in_prev[field, x, own, :]
        for half in range(2):
            x = i if half == 0 else width_x - 1 - i
            for own, size, row in layout.pieces():
                if own is None:
                    cells = [in_border[8 + n, x] for n in range(5)]
                else:
                    cells = [raw[n, x, own, :] for n in range(3)]
                    cells += [raw_int[n, x, own, :].astype(F32) for n in range(2)]
                put_model(natural, half, own.start if own else width_y, size, cells)
        spread_model(coef, natural, i, layout)
        return 0

    for c in range(CHUNKS):
        for copy in loads[c]:
            copy.wait()
        if c + 2 < CHUNKS:
            load(c + 2)
        lax.fori_loop(c * chunk, (c + 1) * chunk, fill, 0)
    out = copies([(coef.at[:, pl.ds(0, ITERS)], edge_c)], sems, 9)
    seam(fa, half_x - 1, rows)
    bufs = (fa, fb)
    covered = cover[0, 0, 0].astype(F32)
    scales = [jnp.where(odd == half, covered, covered / ITERS) for half in range(2)]

    def give_wave(i, half):
        x = i if half == 0 else width_x - 1 - i
        return pltpu.make_async_copy(in_now.at[:, x], wave.at[0, :, x], wave_sems.at[half * half_x + i])

    def finished(step):
        flat = flat_view(bufs[1 - step % 2])

        def done(i):
            for half in range(2):
                x = i if half == 0 else width_x - 1 - i
                for own in layout.tiles():
                    product = products(flat, layout, i, half, own)
                    total = product if step == 0 else corr[x, own, :] + product
                    corr[x, own, :] = scales[half] * total if step == ITERS - 1 else total
                    if step == ITERS - 1:
                        for field in range(4):
                            spot = layout.flat(i, layout.own + own.start, slot(half, field), TILE)
                            in_now[field, x, own, :] = flat[spot, :]
                if step == ITERS - 1:
                    give_wave(i, half).start()

        return done

    for step in range(ITERS):
        old, new = bufs[step % 2], bufs[1 - step % 2]
        sweep(old, new, slopes, sums, coef, (1 + step, half_x), layout, step, finished(step))
        if step < ITERS - 1:
            seam(new, half_x - 1, rows)
        if step == ITERS - 3:
            out += copies([(fa.at[pl.ds(0, ITERS)], edge_a)], sems, 10)
        if step == ITERS - 2:
            far = pl.ds(width_x - ITERS, ITERS)
            out += copies(
                [
                    (fb.at[pl.ds(0, ITERS + 1)], edge_b),
                    (corr.at[pl.ds(0, ITERS)], edge_corr.at[0]),
                    (corr.at[far], edge_corr.at[1]),
                ],
                sems,
                11,
            )
    part = half_x - ITERS
    out += copies(
        [
            (corr.at[pl.ds(ITERS + part * odd, part)], kept),
            (corr.at[pl.ds(ITERS + part * (1 - odd), part)], sent),
        ],
        sems,
        14,
    )
    for copy in out:
        copy.wait()
    for i in range(ITERS, half_x):
        for half in range(2):
            give_wave(i, half).wait()


def border_kernel(
    cover, edge_a, edge_b, edge_c, edge_corr, near, far, corner, wave_in,
    wave, image, image_own,
    fa, fb, slopes, sums, coef, corr, sides, corners, natural, in_now, picture, sems,
):
    second, odd = lax.axis_index("gy"), lax.axis_index("gx") % 2
    width_x, width_y = wave.shape[2], wave.shape[3]
    layout = Rows(width_y, second)
    rows = layout.total
    parts = []
    for begin, end in ((0, ITERS // 2), (ITERS // 2, ITERS)):
        more = (begin + 1 if begin else 0, end + 1)
        parts.append(
            [
                (edge_a.at[pl.ds(begin, end - begin)], fa.at[pl.ds(ITERS + begin, end - begin)]),
                (edge_b.at[pl.ds(more[0], more[1] - more[0])], fb.at[pl.ds(ITERS + more[0], more[1] - more[0])]),
                (edge_c.at[:, pl.ds(begin, end - begin)], coef.at[:, pl.ds(ITERS + begin, end - begin)]),
            ]
        )
    loads = copies(
        [
            (near, sides.at[1 - odd]),
            (far, sides.at[odd]),
            (corner.at[0], corners.at[1 - odd]),
            (corner.at[1], corners.at[odd]),
            (edge_corr, corr),
        ]
        + parts[0]
        + parts[1],
        sems,
    )
    clear_ends([ref.at[pl.ds(0, ITERS)] for ref in (fa, fb)], rows)
    for copy in loads[:4]:
        copy.wait()
    n_now, n_prev, less = 4 * ITERS, 4 * (ITERS - 1), ITERS - 1

    def cells(half, index, own):
        return corners[half, index] if own is None else sides[half, index, own, :]

    def fill(j, _):
        for half in range(2):
            nth = j if half == 0 else ITERS - 1 - j
            shorter = jnp.maximum(j - 1, 0) if half == 0 else jnp.minimum(ITERS - 1 - j, less - 1)
            for own, size, row in layout.pieces():
                for field in range(4):
                    spot = layout.flat(j, row, slot(half, field), size)
                    flat_view(fa)[spot, :] = cells(half, field * ITERS + nth, own)
                    flat_view(fb)[spot, :] = cells(half, n_now + field * less + shorter, own)
        for half in range(2):
            shorter = jnp.maximum(j - 1, 0) if half == 0 else jnp.minimum(ITERS - 1 - j, less - 1)
            for own, size, row in layout.pieces():
                raw = [cells(half, n_now + n_prev + n * less + shorter, own) for n in range(5)]
                put_model(natural, half, own.start if own else width_y, size, raw)
        spread_model(coef, natural, j, layout)
        return 0

    lax.fori_loop(0, ITERS, fill, 0)
    for copy in loads[4:8]:
        copy.wait()

    corr[0, 0] = jnp.zeros(corr.shape[2:], F32)
    corr[1, ITERS - 1] = jnp.zeros(corr.shape[2:], F32)

    def finished(flat):
        def done(i):
            @pl.when(i >= ITERS)
            def _():
                for half in range(2):
                    x = i - ITERS if half == 0 else 2 * ITERS - 1 - i
                    for own in layout.tiles():
                        corr[half, x, own, :] = corr[half, x, own, :] + products(flat, layout, i, half, own)

        return done

    def advance(turn, _):
        @pl.when(turn == 1)
        def _():
            for copy in loads[8:]:
                copy.wait()

        for step, (old, new) in enumerate(((fa, fb), (fb, fa))):
            start = 1 + step + 2 * turn
            sweep(old, new, slopes, sums, coef, (start, start + ITERS), layout, step, finished(flat_view(new)))
        return 0

    lax.fori_loop(0, ITERS // 2, advance, 0)
    corr[...] = cover[0, 0, 0].astype(F32) * corr[...]
    picture[...] = corr[...] * (1.0 / ITERS)
    out = copies([(picture, image), (corr, image_own)], sems)
    flat = flat_view(fa)

    def give(i, _):
        for half in range(2):
            x = i if half == 0 else ITERS - 1 - i
            for own in layout.tiles():
                for field in range(4):
                    spot = layout.flat(ITERS + i, layout.own + own.start, slot(half, field), TILE)
                    in_now[half, field, x, own, :] = flat[spot, :]
        return 0

    lax.fori_loop(0, ITERS, give, 0)
    out += copies(
        [
            (in_now.at[0], wave.at[0, :, pl.ds(0, ITERS)]),
            (in_now.at[1], wave.at[0, :, pl.ds(width_x - ITERS, ITERS)]),
        ],
        sems,
        2,
    )
    for copy in out:
        copy.wait()


def any_specs(count):
    return [pl.BlockSpec(memory_space=pl.ANY)] * count


MIB = 1024 * 1024


def pack_kernel(
    now, prev, vel, eps, delta, tilt, azimuth,
    near_out, far_out, border_out,
    near, far, border, planes_int, wave_rows, float_rows, int_rows, sems,
):
    second, odd = lax.axis_index("gy"), lax.axis_index("gx") % 2
    width_x, width_y = vel.shape[0], vel.shape[1]
    deep, less = ITERS, ITERS - 1
    n_now, n_prev = 4 * deep, 4 * less
    ints, floats = (tilt, azimuth), (vel, eps, delta)
    tile = pl.ds(pl.multiple_of((1 - second) * (width_y - TILE), TILE), TILE)
    pairs = []
    ends = ((near, 1 - odd), (far, odd))
    for k, (_, high) in enumerate(ends):
        at = pl.ds(high * (width_x - less), less)
        pairs += [(ints[n].at[at], planes_int.at[k, n]) for n in range(2)]
    for out, high in ends:
        at = pl.ds(high * (width_x - less), less)
        for f in range(4):
            pairs.append((now.at[0, f, pl.ds(high * (width_x - deep), deep)], out.at[pl.ds(f * deep, deep)]))
            pairs.append((prev.at[0, f, at], out.at[pl.ds(n_now + f * less, less)]))
        for n in range(3):
            pairs.append((floats[n].at[at], out.at[pl.ds(n_now + n_prev + n * less, less)]))
    planes = len(pairs)
    pairs += [(array.at[0, :, :, tile], wave_rows.at[n]) for n, array in enumerate((now, prev))]
    pairs += [(array.at[:, tile], float_rows.at[n]) for n, array in enumerate(floats)]
    pairs += [(array.at[:, tile], int_rows.at[n]) for n, array in enumerate(ints)]
    started = copies(pairs, sems)
    for copy in started[:planes]:
        copy.wait()
    for k, (out, _) in enumerate(ends):
        for n in range(2):
            begin = n_now + n_prev + (3 + n) * less
            out[begin : begin + less] = planes_int[k, n].astype(F32)

    given = copies([(near, near_out), (far, far_out)], sems, len(pairs))
    for copy in started[planes:]:
        copy.wait()

    def needed(ref, *spot):
        return ref[spot + (pl.ds(REACH * (1 - second), REACH), slice(None))]

    def rows(x, _):
        for kind in range(2):
            for f in range(4):
                border[4 * kind + f, x] = needed(wave_rows, kind, f, x)
        for n in range(3):
            border[8 + n, x] = needed(float_rows, n, x)
        for n in range(2):
            border[11 + n, x] = needed(int_rows, n, x).astype(F32)
        return 0

    lax.fori_loop(0, width_x // 4, lambda x, _: [rows(4 * x + i, 0) for i in range(4)][0], 0)
    for copy in given + copies([(border, border_out)], sems, len(pairs) + 2):
        copy.wait()


def pack(now, prev, vel, eps, delta, tilt, azimuth):
    width_x, width_y = vel.shape[0], vel.shape[1]
    planes = 4 * ITERS + 9 * (ITERS - 1)
    face = jax.ShapeDtypeStruct((planes, width_y, LANES), F32)
    return pl.pallas_call(
        pack_kernel,
        in_specs=any_specs(7),
        out_specs=any_specs(3),
        out_shape=(face, face, jax.ShapeDtypeStruct((13, width_x, REACH, LANES), F32)),
        scratch_shapes=[
            pltpu.VMEM(face.shape, F32),
            pltpu.VMEM(face.shape, F32),
            pltpu.VMEM((13, width_x, REACH, LANES), F32),
            pltpu.VMEM((2, 2, ITERS - 1, width_y, LANES), jnp.int32),
            pltpu.VMEM((2, 4, width_x, TILE, LANES), F32),
            pltpu.VMEM((3, width_x, TILE, LANES), F32),
            pltpu.VMEM((2, width_x, TILE, LANES), jnp.int32),
            pltpu.SemaphoreType.DMA((36,)),
        ],
        compiler_params=pltpu.CompilerParams(vmem_limit_bytes=60 * MIB),
        cost_estimate=pl.CostEstimate(flops=1_000_000, bytes_accessed=8_000_000, transcendentals=0),
        name="pack_borders",
    )(now, prev, vel, eps, delta, tilt, azimuth)


def advance_inner(cover, now, prev, vel, eps, delta, tilt, azimuth, border):
    width_x, width_y = vel.shape[0], vel.shape[1]
    rows = width_y + REACH + 2
    half_x = width_x // 2
    shape = functools.partial(jax.ShapeDtypeStruct, dtype=F32)
    block = (half_x + 1, rows, SLOTS, LANES)
    part = shape((half_x - ITERS, width_y, LANES))
    vmem = lambda size: pltpu.VMEM(size, F32)
    return pl.pallas_call(
        inner_kernel,
        in_specs=[pl.BlockSpec(memory_space=pltpu.SMEM)] + any_specs(8),
        out_specs=any_specs(7),
        out_shape=(
            shape(now.shape),
            shape((ITERS,) + block[1:]),
            shape((ITERS + 1,) + block[1:]),
            shape((FACTORS, ITERS) + block[1:]),
            shape((2, ITERS, width_y, LANES)),
            part,
            part,
        ),
        scratch_shapes=[vmem(block)] * 4
        + [
            vmem((FACTORS, half_x) + block[1:]),
            vmem(vel.shape),
            vmem(now.shape[1:]),
            vmem(now.shape[1:]),
            vmem((3, width_x, width_y, LANES)),
            pltpu.VMEM((2, width_x, width_y, LANES), jnp.int32),
            vmem(border.shape),
            vmem((2, FACTORS + 1, rows + TILE, LANES)),
            pltpu.SemaphoreType.DMA((CHUNKS, 15)),
            pltpu.SemaphoreType.DMA((16,)),
            pltpu.SemaphoreType.DMA((width_x,)),
        ],
        compiler_params=pltpu.CompilerParams(vmem_limit_bytes=60 * MIB),
        cost_estimate=pl.CostEstimate(flops=80_000_000, bytes_accessed=200_000_000, transcendentals=0),
        name="inner_steps",
    )(cover, now, prev, vel, eps, delta, tilt, azimuth, border)


def advance_border(cover, edge_a, edge_b, edge_c, edge_corr, near, far, corner, wave):
    width_y = wave.shape[3]
    rows = width_y + REACH + 2
    block = (2 * ITERS + 1, rows, SLOTS, LANES)
    shape = functools.partial(jax.ShapeDtypeStruct, dtype=F32)
    vmem = lambda size: pltpu.VMEM(size, F32)
    return pl.pallas_call(
        border_kernel,
        in_specs=[pl.BlockSpec(memory_space=pltpu.SMEM)] + any_specs(8),
        out_specs=any_specs(3),
        out_shape=(shape(wave.shape), shape(edge_corr.shape), shape(edge_corr.shape)),
        scratch_shapes=[vmem(block)] * 4
        + [
            vmem((FACTORS,) + block),
            vmem(edge_corr.shape),
            vmem((2,) + near.shape),
            vmem(corner.shape),
            vmem((2, FACTORS + 1, rows + TILE, LANES)),
            vmem((2, 4, ITERS, width_y, LANES)),
            vmem(edge_corr.shape),
            pltpu.SemaphoreType.DMA((11,)),
        ],
        input_output_aliases={8: 0},
        compiler_params=pltpu.CompilerParams(vmem_limit_bytes=60 * MIB),
        cost_estimate=pl.CostEstimate(flops=20_000_000, bytes_accessed=20_000_000, transcendentals=0),
        name="border_steps",
    )(cover, edge_a, edge_b, edge_c, edge_corr, near, far, corner, wave)


def cut(array, start, size, axis):
    return lax.dynamic_slice_in_dim(array, start, size, axis=axis)


def other_rows(block, axis, second):
    return cut(block, (1 - second) * (block.shape[axis] - REACH), REACH, axis)


def swap_cores(rows):
    return lax.ppermute(rows, "gy", [(0, 1), (1, 0)])


def pairs_at(distance):
    return [(i, i ^ distance) for i in range(lax.axis_size("shot"))]


def scaled(block):
    return lax.optimization_barrier(block * (1.0 / ITERS))


def local(wave_now, wave_prev, vel_coef, epsilon, delta, tilt, azimuth, aperture):
    second = lax.axis_index("gy")
    columns = lax.axis_size("gx")
    inputs = (wave_now, wave_prev, vel_coef, epsilon, delta, tilt, azimuth)
    near, far, border = pack(*inputs)
    near = lax.ppermute(near, "gx", [(i, i ^ 1) for i in range(columns) if i ^ 1 < columns])
    border = swap_cores(border)
    far, border = lax.optimization_barrier((far, border))
    far = lax.ppermute(far, "gx", [(i, j) for i in range(1, columns - 1) for j in [i + 1 if i % 2 else i - 1]])
    wave, edge_a, edge_b, edge_c, edge_corr, kept, sent = advance_inner(aperture, *inputs, border)
    received = lax.ppermute(sent, "shot", pairs_at(1))
    mine = scaled(kept)
    received, near, far = lax.optimization_barrier((received, near, far))
    corner = swap_cores(jnp.stack([other_rows(f, 1, second) for f in (near, far)]))
    received, corner = lax.optimization_barrier((received, corner))
    held = mine + received
    held, edge_corr = lax.optimization_barrier((held, edge_corr))
    wave, outside, outside_own = advance_border(aperture, edge_a, edge_b, edge_c, edge_corr, near, far, corner, wave)
    distance = 2
    while distance < lax.axis_size("shot"):
        held = held + lax.ppermute(held, "shot", pairs_at(distance))
        distance *= 2
    held, outside_own = lax.optimization_barrier((held, outside_own))
    own, distance = scaled(outside_own), 1
    while distance < lax.axis_size("shot"):
        own = outside = own + lax.ppermute(outside, "shot", pairs_at(distance))
        if distance == 1:
            held, own, outside = lax.optimization_barrier((held, own, outside))
            other = lax.ppermute(held, "shot", pairs_at(1))
        distance *= 2
    even = lax.axis_index("shot") % 2 == 0
    first, then = jnp.where(even, held, other), jnp.where(even, other, held)
    return wave, jnp.concatenate([outside[0], first, then, outside[1]])


def solution(mesh):
    return jax.shard_map(
        local,
        mesh=mesh,
        in_specs=(
            P("shot", None, "gx", "gy", None),
            P("shot", None, "gx", "gy", None),
            P("gx", "gy", None),
            P("gx", "gy", None),
            P("gx", "gy", None),
            P("gx", "gy", None),
            P("gx", "gy", None),
            P("shot", "gx", "gy"),
        ),
        out_specs=(P("shot", None, "gx", "gy", None), P("gx", "gy", None)),
        check_vma=False,
    )
```
